128 devices in a mesh: sec: 4 (over x), dev: 32 (over z, y, core).
Axes of the slice: x: 4, y: 4, z: 4, core: 2. Of those that a mesh axis runs over, the one named last changes fastest.
Arguments:
- strain_rows: bfloat16 [262144, 128], P(('sec', 'dev')), may hold values from -6 to 6
- bands: int32 [262144], P(('sec', 'dev')), may hold values from 0 to 15
- damaged: int32 [16384], P(('sec', 'dev')), may hold values from 0 to 2047
- owner: int32 [16384, 1], P(('sec', 'dev')), may hold values from 0 to 127; in each aligned block of 128 rows (0 to 127, 128 to 255, ...) at most 2 rows name the same one
- first_layers: bfloat16 [16384, 4096], P(('sec', 'dev')), may hold values from -0.5 to 0.5
- middle_weight: bfloat16 [4096, 4096], P(None, 'sec'), may hold values from -0.09375 to 0.09375
- out_weight: bfloat16 [4096, 128], P('sec'), may hold values from -0.09375 to 0.09375
- band_scale: float32 [16, 4096], replicated, may hold values from 0.5 to 2
- back_weight: bfloat16 [128, 128], replicated, may hold values from -0.5 to 0.5
Outputs:
- response: bfloat16 [16384, 128], P(('sec', 'dev'))
The draws below stay inside these ranges and needn't reach their ends.
Inputs may be any that keep to these rules, and one draw needn't show every extreme that they name: Among the 128 rows of one macro device no owner is named more than 2 times, a bound that some block reaches. `damaged`: indices into the listing device's own 2048 points.
All inputs are finite; a program needn't handle non-finite values.
Results may differ from the reference program's by a relative error of at most 0.014.
Values may be sent and summed in bfloat16 or wider, within the bound.
A program may use at most 128 MiB of HBM per device.

```python
import math
import jax
import jax.numpy as jnp
import numpy as np
from jax import lax

FEAT = 128
HID = 4096
OUT = 128
BANDS = 16
P_DEV = 2048
LIST_DEV = 128
PASSES = 2
POINTS = 262144
LISTED = 16384
CAP = 2
RECV = 256
DEVICES = 128


def touch_ends(entries, own_key, least, top_value):
    shape = entries.shape
    index_at = [jax.random.randint(jax.random.fold_in(own_key, axis), (), 0, shape[axis]) for axis in range(len(shape))]
    entries = entries.at[tuple(index_at)].set(least)
    longest = shape.index(max(shape))
    index_at[longest] = (index_at[longest] + 1) % shape[longest]
    return entries.at[tuple(index_at)].set(top_value)


def level_of(own_key, extent, cuts, smallest, largest):
    factor_of, own = 1.0, jax.random.fold_in(own_key, 6)
    for dim, parts in cuts:
        draws = jnp.exp(jax.random.uniform(jax.random.fold_in(own, dim), (parts,), jnp.float32, smallest / len(cuts), largest / len(cuts)))
        factor_of = factor_of * jnp.repeat(draws, extent[dim] // parts).reshape([-1 if axis == dim else 1 for axis in range(len(extent))])
    return factor_of


def shared_out(key, own, number, rows, number_of, top, reach, skew):
    sequence = jax.random.permutation(key, number_of)
    crowded, ordinary = load_shares(number_of, rows * top, reach, skew, True), load_shares(number_of, rows * top, reach, skew, False)
    places = jnp.arange(number_of)

    def named(tallies, rotation):
        used = int((tallies > 0).sum())
        fixed = max(1, used // 4)
        passed = fixed + (places - fixed + rotation * (used - fixed)) % max(1, number_of - fixed)
        return jnp.zeros((number_of,), jnp.int32).at[sequence[jnp.where(places < fixed, places, passed)]].set(jnp.asarray(tallies, jnp.int32))

    tallies = jnp.where(number % 4 == 0, named(crowded, number // 4), named(ordinary, number - number // 4 - 1))
    mixed = jax.random.permutation(jax.random.fold_in(own, 3), number_of)
    donor, taker = mixed[0:number_of // 2 * 2:2], mixed[1:number_of // 2 * 2:2]
    slack = jnp.minimum(tallies[donor] - 1, reach - tallies[taker]) // 2
    slack = jnp.where((donor == sequence[0]) | (taker == sequence[0]) | (tallies[taker] == 0), 0, jnp.maximum(slack, 0))
    passed = jax.random.randint(jax.random.fold_in(own, 4), (number_of // 2,), 0, 1 << 20) % (slack + 1)
    tallies = tallies.at[donor].add(-passed).at[taker].add(passed)
    labels = jnp.searchsorted(jnp.cumsum(tallies), jnp.arange(rows * top), side="right").astype(jnp.int32)
    listing = labels.reshape(top, rows).T
    listing = listing[jax.random.permutation(jax.random.fold_in(own, 1), rows)]
    rotation = jax.random.randint(jax.random.fold_in(own, 2), (rows, 1), 0, top)
    return jnp.take_along_axis(listing, (jnp.arange(top)[None, :] + rotation) % top, axis=1)


def load_shares(number_of, total, most, skew, full):
    weights = [(1 << 20) // math.isqrt(standing ** skew) + 1 for standing in range(1, number_of + 1)]
    largest = most if full else min(most, max(-(-total // number_of), total * weights[0] // sum(weights)))
    least = 1 if total - largest >= number_of - 1 else 0
    given, surplus = [largest] + [least] * (number_of - 1), total - largest - least * (number_of - 1)
    while surplus > 0:
        free = [i for i in range(1, number_of) if given[i] < largest] or [i for i in range(1, number_of) if given[i] < most]
        pool, budget = sum([weights[i] for i in free]), surplus
        for i in free:
            more = min(most - given[i], max(1, budget * weights[i] // pool), surplus)
            given[i] = given[i] + more
            surplus = surplus - more
    return np.array(given)


def noise(key, dims, deviation, reach, pieces=(), kind=jnp.bfloat16):
    values = jax.random.normal(key, dims, jnp.float32) * deviation
    if len(pieces) > 0:
        values = level_of(key, dims, pieces, -0.22, 0.18) * values
    return jnp.clip(values, min=-reach, max=reach).astype(kind)


def setup_inputs(seed: int = 0) -> dict:
    streams_of = jax.random.split(jax.random.key(seed), 10)
    strain_rows = noise(streams_of[0], (POINTS, FEAT), 1.0, 6.0, ((0, 128),))
    bands = touch_ends(jax.random.randint(streams_of[1], (POINTS,), 0, BANDS), jax.random.fold_in(streams_of[1], 1), 0, BANDS - 1).astype(jnp.int32)
    damaged = touch_ends(jax.random.randint(streams_of[2], (LISTED,), 0, P_DEV), jax.random.fold_in(streams_of[2], 1), 0, P_DEV - 1).astype(jnp.int32)
    owner_keys = jax.random.split(jax.random.fold_in(streams_of[3], 1), LISTED // LIST_DEV)
    owner_turns = jax.random.permutation(jax.random.fold_in(streams_of[3], 3), LISTED // LIST_DEV)
    owner = jax.vmap(lambda own, number: shared_out(jax.random.fold_in(streams_of[3], 2), own, number, LIST_DEV, DEVICES, 1, CAP, 2))(owner_keys, owner_turns).reshape((LISTED, 1))
    first_layers = noise(streams_of[4], (DEVICES * FEAT, HID), FEAT ** -0.5, 0.5, ((0, 128),))
    middle_weight = noise(streams_of[5], (HID, HID), HID ** -0.5, 0.09375, ((1, 4),))
    out_weight = noise(streams_of[6], (HID, OUT), HID ** -0.5, 0.09375, ((0, 4),))
    band_scale = jnp.clip(jnp.exp(jax.random.uniform(streams_of[7], (BANDS, HID), jnp.float32, math.log(0.5), math.log(2.0))), 0.5, 2.0)
    back_weight = noise(streams_of[8], (OUT, FEAT), OUT ** -0.5, 0.5)
    return dict(strain_rows=strain_rows, bands=bands, damaged=damaged, owner=owner, first_layers=first_layers, middle_weight=middle_weight, out_weight=out_weight, band_scale=band_scale, back_weight=back_weight)


def reference(strain_rows, bands, damaged, owner, first_layers, middle_weight, out_weight, band_scale, back_weight):
    listed = damaged.shape[0]
    point_index = (jnp.arange(listed, dtype=jnp.int32) // LIST_DEV) * P_DEV + damaged.astype(jnp.int32)
    features = strain_rows[point_index]
    point_band = bands[point_index]
    owners = owner[:, 0].astype(jnp.int32)
    ordering = jnp.argsort(owners, stable=True).astype(jnp.int32)
    counts = jnp.sum((owners[None, :] == jnp.arange(DEVICES, dtype=jnp.int32)[:, None]).astype(jnp.int32), axis=1)
    starts = jnp.cumsum(counts) - counts
    slot_index = jnp.arange(RECV, dtype=jnp.int32)
    position = jnp.minimum(starts[:, None] + slot_index[None, :], listed - 1).astype(jnp.int32)
    live_slot = slot_index[None, :] < counts[:, None]
    row_index = ordering[position]
    owner_weights = first_layers.reshape(DEVICES, FEAT, HID)
    target_rows = jnp.where(live_slot, row_index, listed).reshape(-1)
    result = None
    for segment_index in range(PASSES):
        def first_part(packed):
            weight_block, row_ids = packed
            block_rows = features[row_ids]
            scale_rows = band_scale[point_band[row_ids]]
            mixed = jnp.dot(block_rows, weight_block, preferred_element_type=jnp.float32) * scale_rows
            return jax.nn.silu(mixed).astype(jnp.bfloat16)

        per_owner = lax.map(first_part, (owner_weights, row_index))
        hidden = jnp.zeros((listed, HID), per_owner.dtype).at[target_rows].set(per_owner.reshape(-1, HID), mode="drop")

        def rest_part(hidden_block):
            middle = jax.nn.silu(jnp.dot(hidden_block, middle_weight, preferred_element_type=jnp.float32)).astype(jnp.bfloat16)
            return jnp.dot(middle, out_weight, preferred_element_type=jnp.float32).astype(jnp.bfloat16)

        result = lax.map(rest_part, hidden.reshape(listed // LIST_DEV, LIST_DEV, HID)).reshape(listed, OUT)
        features = (features.astype(jnp.float32) + jnp.dot(result, back_weight, preferred_element_type=jnp.float32)).astype(jnp.bfloat16)
    return result
```

```python
import functools

import jax
import jax.numpy as jnp
from jax import lax
from jax.experimental import pallas as pl
from jax.experimental.pallas import tpu as pltpu
from jax.sharding import PartitionSpec as P

MESH = pl.DeviceIdType.MESH
BF = jnp.bfloat16
F32 = jnp.float32
CHUNKS = 4


def iota(shape, axis):
    return lax.broadcasted_iota(jnp.int32, shape, axis)


def mm(a, b):
    return jnp.dot(a, b, preferred_element_type=F32)


def hot(cond):
    return jnp.where(cond, 1.0, 0.0).astype(BF)


def half_silu(u):
    return u + u * jnp.tanh(u)


def wait_bytes(ref, sem):
    pltpu.make_async_copy(ref, ref, sem).wait()


def kernel(
    nx,
    nd,
    strain_hbm,
    bands_ref,
    damaged_ref,
    owner_ref,
    w1_hbm,
    w2_hbm,
    outw_ref,
    scale_ref,
    back_ref,
    out_ref,
    strain_v,
    w1_v,
    w2_v,
    scale_v,
    scales_v,
    gather_v,
    dispatch_v,
    combine_v,
    feats_v,
    x0_v,
    x1_v,
    s0_v,
    s1_v,
    a0_v,
    a1_v,
    xw_v,
    h_v,
    acc_v,
    r0_v,
    r1_v,
    t0_v,
    t1_v,
    y0_v,
    y1_v,
    local_sem,
    w1own_sem,
    w1send_sem,
    w1recv_sem,
    send_sem,
    recv_sem,
):
    x = lax.axis_index("sec")
    d = lax.axis_index("dev")
    barrier = pltpu.get_barrier_semaphore()
    n = 128
    ch = w1_v.shape[3]
    right, left = lax.rem(x + 1, nx), lax.rem(x + nx - 1, nx)

    def at_x(k):
        return lax.rem(x + k, nx)

    for k in range(1, nx):
        pl.semaphore_signal(barrier, inc=1, device_id=(at_x(k), d), device_id_type=MESH)

    @pl.loop(1, nd)
    def _(i):
        pl.semaphore_signal(
            barrier, inc=1, device_id=(x, lax.rem(d + i, nd)), device_id_type=MESH
        )

    strain_copy = pltpu.make_async_copy(strain_hbm, strain_v, local_sem.at[0])
    strain_copy.start()
    w2_copy = pltpu.make_async_copy(w2_hbm, w2_v, local_sem.at[1])
    w2_copy.start()
    own_copies = []
    for c in range(CHUNKS):
        own = pltpu.make_async_copy(
            w1_hbm.at[:, pl.ds(c * ch, ch)], w1_v.at[c, 0], w1own_sem.at[c]
        )
        own.start()
        own_copies.append(own)

    eye = iota((n, n), 0) == iota((n, n), 1)
    ones = jnp.ones((n, n), BF)

    def spread(row):
        return mm(jnp.where(eye, row, 0.0).astype(BF), ones)

    damaged = damaged_ref[...]
    high = spread((damaged // n).astype(F32))
    low = spread((damaged % n).astype(F32))
    lane = iota((n, n), 1).astype(F32)
    on_low = low == lane
    band_part = jnp.zeros((n, n), F32)
    for b in range(strain_v.shape[0] // n):
        picked = jnp.logical_and(on_low, high == float(b))
        gather_v[:, b * n : (b + 1) * n] = hot(picked)
        band_part += jnp.where(picked, bands_ref[b : b + 1, :].astype(F32), 0.0)
    band_spread = mm(band_part.astype(BF), ones)
    band_row = jnp.sum(jnp.where(eye, band_spread, 0.0), axis=0, keepdims=True)
    owner_row = owner_ref[...].astype(F32)
    earlier = jnp.logical_and(
        spread(owner_row) == owner_row, iota((n, n), 0) < iota((n, n), 1)
    )
    rank = jnp.sum(jnp.where(earlier, 1.0, 0.0), axis=0, keepdims=True)
    target_row = 2.0 * owner_row + rank
    meta_at = iota((16, n), 0)
    x0_v[0, n : n + 16, :] = jnp.where(
        meta_at == 0, target_row, jnp.where(meta_at == 1, band_row, 0.0)
    ).astype(BF)
    strain_copy.wait()
    feats = mm(gather_v[...], strain_v[...])
    feats_v[...] = feats
    x0_v[0, 0:n, :] = feats.astype(BF)

    half = scale_ref[...] * 0.5
    term0 = half.astype(BF)
    rest = half - term0.astype(F32)
    term1 = rest.astype(BF)
    term2 = (rest - term1.astype(F32)).astype(BF)
    scale_v[0:16, :] = term0
    scale_v[16:32, :] = term1
    scale_v[32:48, :] = term2
    scale_v[48:128, :] = jnp.zeros((80, scale_v.shape[1]), BF)

    pl.semaphore_wait(barrier, nx - 1 + nd - 1)

    def send_along_x(src_of, dst, sem):
        for k in range(1, nx):
            pltpu.make_async_remote_copy(
                src_ref=src_of(k),
                dst_ref=dst.at[(nx - k) % nx],
                send_sem=send_sem.at[sem],
                recv_sem=recv_sem.at[sem],
                device_id=(at_x(k), d),
                device_id_type=MESH,
            ).start()

    def send_all(src, dst, sem):
        @pl.loop(1, nd)
        def _(i):
            to = lax.rem(d + i, nd)
            pltpu.make_async_remote_copy(
                src_ref=src.at[to],
                dst_ref=dst.at[d],
                send_sem=send_sem.at[sem],
                recv_sem=recv_sem.at[sem],
                device_id=(x, to),
                device_id_type=MESH,
            ).start()

        dst[pl.ds(d, 1)] = src[pl.ds(d, 1)]

    send_along_x(lambda k: x0_v.at[0], x0_v, 0)

    def w1_copy(src, c, slot, to, sem):
        return pltpu.make_async_remote_copy(
            src_ref=src,
            dst_ref=w1_v.at[c, slot],
            send_sem=w1send_sem.at[sem, c],
            recv_sem=w1recv_sem.at[slot, c],
            device_id=(to, d),
            device_id_type=MESH,
        )

    w1_copies = {}
    for c in range(CHUNKS):
        src = w1_hbm.at[:, pl.ds(c * ch, ch)]
        w1_copies[1, c] = w1_copy(src, c, 1, left, 0)
        w1_copies[3, c] = w1_copy(src, c, 3, right, 1)
        w1_copies[1, c].start()
        w1_copies[3, c].start()
        if c % 2 == 0:
            w1_copies[2, c] = w1_copy(w1_v.at[c, 3], c, 2, right, 2)
        else:
            w1_copies[2, c] = w1_copy(w1_v.at[c, 1], c, 2, left, 2)

    rows = nd * 32
    wait_bytes(x0_v.at[pl.ds(1, nx - 1)], recv_sem.at[0])

    def slot_code(at):
        dest, owner_at = at // 32, (at // 8) % 4
        lister, slot = (at // 2) % 4, at % 2
        code = (lax.rem(x + owner_at, nx) * nd + dest) * 2 + slot
        return code, lister

    down, down_lister = slot_code(iota((rows, n), 0))
    along, along_lister = slot_code(iota((n, rows), 1))
    band_cols = []
    for j in range(nx):
        meta = x0_v[j, n : n + 16, :].astype(F32)
        target_j, band_j = meta[0:1, :], meta[1:2, :]
        dispatch_v[:, j * n : (j + 1) * n] = hot(
            jnp.where(down_lister == j, down, -1).astype(F32) == target_j
        )
        target_down = spread(target_j)
        for b in range(rows // n):
            cut = slice(b * n, (b + 1) * n)
            combine_v[j * n : (j + 1) * n, cut] = hot(
                jnp.where(along_lister[:, cut] == j, along[:, cut], -1).astype(F32)
                == target_down
            )
        band_cols.append(spread(band_j).astype(BF))
    bands_all = jnp.concatenate(band_cols, axis=0)

    def spread_rows(features):
        return mm(dispatch_v[...], features).astype(BF).reshape(nd, 32, n)

    s0_v[:, 0:32, :] = spread_rows(x0_v[:, 0:n, :].reshape(nx * n, n))
    s0_v[:, 32:64, :] = spread_rows(bands_all)
    send_all(s0_v, a0_v, 1)
    wait_bytes(a0_v.at[pl.ds(0, nd - 1)], recv_sem.at[1])

    pair_rows = nd * 16
    level = iota((pair_rows, n), 1)
    level_of = jnp.where(level < 48, level % 16, -1).astype(F32)
    for p in range(2):
        got = a0_v[:, 32 + 16 * p : 48 + 16 * p, :].reshape(pair_rows, n).astype(F32)
        picks = hot(got == level_of)

        @pl.loop(0, scale_v.shape[1] // 256)
        def _(t):
            cols = pl.ds(pl.multiple_of(t * 256, 256), 256)
            scales_v[p, :, cols] = mm(picks, scale_v[:, cols])

    def widen(got, p):
        which = (iota((pair_rows, n), 0) // 8) % 2
        value = got[:, 16 * p : 16 * p + 16, :].reshape(pair_rows, n)
        zero = jnp.zeros_like(value)
        xw_v[p, :, 0:n] = jnp.where(which == 0, value, zero)
        xw_v[p, :, n : 2 * n] = jnp.where(which == 1, value, zero)

    def chunk(p, c):
        @pl.loop(0, ch // 256)
        def _(t):
            cols = pl.ds(pl.multiple_of(t * 256, 256), 256)
            across = pl.ds(pl.multiple_of(c * ch + t * 256, 256), 256)
            layer = w1_v[c, 2 * p : 2 * p + 2, :, cols].reshape(2 * n, 256)
            u = mm(xw_v[p], layer) * scales_v[p, :, across]
            h_v[:, cols] = half_silu(u).astype(BF)

        @pl.loop(0, w2_v.shape[1] // 256)
        def _(t):
            cols = pl.ds(pl.multiple_of(t * 256, 256), 256)
            part = mm(h_v[...], w2_v[c * ch : (c + 1) * ch, cols])
            if c == 0:
                acc_v[p, :, cols] = part
            else:
                acc_v[p, :, cols] += part

    def tail(p, dst):
        total = jnp.zeros((pair_rows, n), F32)
        for t in range(w2_v.shape[1] // 256):
            cols = slice(t * 256, (t + 1) * 256)
            middle = half_silu(acc_v[p, :, cols] * 0.5).astype(BF)
            total += mm(middle, outw_ref[cols, :])
        dst[:, 16 * p : 16 * p + 16, :] = total.astype(BF).reshape(nd, 16, n)

    def give_back(r_v, t_v, y_v, sem):
        send_all(r_v, t_v, sem)
        wait_bytes(t_v.at[pl.ds(0, nd - 1)], recv_sem.at[sem])
        points = mm(combine_v[...], t_v[...].reshape(rows, n))
        y_v[...] = points.astype(BF).reshape(nx, n, n)

    def sum_along_x(y_v, y_in, sem):
        send_along_x(lambda k: y_v.at[k], y_in, sem)
        wait_bytes(y_in.at[pl.ds(1, nx - 1)], recv_sem.at[sem])
        total = y_v[0].astype(F32)
        for k in range(1, nx):
            total += y_in[k].astype(F32)
        return total.astype(BF)

    for p in range(2):
        widen(a0_v[:, 0:32, :], p)
    w2_copy.wait()
    for c in range(CHUNKS):
        own_copies[c].wait()
        w1_copies[1, c].wait_recv()
        w1_copies[3, c].wait_recv()
        w1_copies[2, c].start()
        chunk(0, c)
    tail(0, r0_v)
    for c in range(CHUNKS):
        w1_copies[2, c].wait_recv()
        chunk(1, c)
    tail(1, r0_v)
    give_back(r0_v, t0_v, y0_v.at[0], 2)
    values = sum_along_x(y0_v.at[0], y0_v.at[1], 3)
    features = (feats_v[...] + mm(values, back_ref[...])).astype(BF)

    x1_v[0] = features
    send_along_x(lambda k: x1_v.at[0], x1_v, 4)
    wait_bytes(x1_v.at[pl.ds(1, nx - 1)], recv_sem.at[4])
    s1_v[...] = spread_rows(x1_v[...].reshape(nx * n, n))
    send_all(s1_v, a1_v, 5)
    wait_bytes(a1_v.at[pl.ds(0, nd - 1)], recv_sem.at[5])
    for p in range(2):
        widen(a1_v[...], p)
    for p in range(2):
        for c in range(CHUNKS):
            chunk(p, c)
        tail(p, r1_v)
    give_back(r1_v, t1_v, y1_v.at[0], 6)
    out_ref[...] = sum_along_x(y1_v.at[0], y1_v.at[1], 7)

    for copy in w1_copies.values():
        copy.wait_send()
    wait_bytes(x0_v.at[pl.ds(1, nx - 1)], send_sem.at[0])
    wait_bytes(a0_v.at[pl.ds(0, nd - 1)], send_sem.at[1])
    wait_bytes(t0_v.at[pl.ds(0, nd - 1)], send_sem.at[2])
    wait_bytes(y0_v.at[1, pl.ds(1, nx - 1)], send_sem.at[3])
    wait_bytes(x1_v.at[pl.ds(1, nx - 1)], send_sem.at[4])
    wait_bytes(a1_v.at[pl.ds(0, nd - 1)], send_sem.at[5])
    wait_bytes(t1_v.at[pl.ds(0, nd - 1)], send_sem.at[6])
    wait_bytes(y1_v.at[1, pl.ds(1, nx - 1)], send_sem.at[7])


def solution(mesh):
    nx, nd = mesh.shape["sec"], mesh.shape["dev"]

    def per_device(strain, bands, damaged, owner, w1, w2, outw, scale, back):
        n, hid = w1.shape
        points = strain.shape[0]
        mid = w2.shape[1]
        rows = nd * 32
        vmem = pl.BlockSpec(memory_space=pltpu.VMEM)
        hbm = pl.BlockSpec(memory_space=pl.ANY)
        return pl.pallas_call(
            functools.partial(kernel, nx, nd),
            out_shape=jax.ShapeDtypeStruct((n, outw.shape[1]), BF),
            in_specs=[hbm, vmem, vmem, vmem, hbm, hbm, vmem, vmem, vmem],
            out_specs=vmem,
            scratch_shapes=[
                pltpu.VMEM((points, n), BF),
                pltpu.VMEM((CHUNKS, nx, n, hid // CHUNKS), BF),
                pltpu.VMEM((hid, mid), BF),
                pltpu.VMEM((n, hid), BF),
                pltpu.VMEM((2, rows // 2, hid), F32),
                pltpu.VMEM((n, points), BF),
                pltpu.VMEM((rows, nx * n), BF),
                pltpu.VMEM((nx * n, rows), BF),
                pltpu.VMEM((n, n), F32),
                pltpu.VMEM((nx, n + 16, n), BF),
                pltpu.VMEM((nx, n, n), BF),
                pltpu.VMEM((nd, 64, n), BF),
                pltpu.VMEM((nd, 32, n), BF),
                pltpu.VMEM((nd, 64, n), BF),
                pltpu.VMEM((nd, 32, n), BF),
                pltpu.VMEM((2, rows // 2, 2 * n), BF),
                pltpu.VMEM((rows // 2, hid // CHUNKS), BF),
                pltpu.VMEM((2, rows // 2, mid), F32),
                pltpu.VMEM((nd, 32, n), BF),
                pltpu.VMEM((nd, 32, n), BF),
                pltpu.VMEM((nd, 32, n), BF),
                pltpu.VMEM((nd, 32, n), BF),
                pltpu.VMEM((2, nx, n, n), BF),
                pltpu.VMEM((2, nx, n, n), BF),
                pltpu.SemaphoreType.DMA((2,)),
                pltpu.SemaphoreType.DMA((CHUNKS,)),
                pltpu.SemaphoreType.DMA((3, CHUNKS)),
                pltpu.SemaphoreType.DMA((nx, CHUNKS)),
                pltpu.SemaphoreType.DMA((8,)),
                pltpu.SemaphoreType.DMA((8,)),
            ],
            compiler_params=pltpu.CompilerParams(
                collective_id=0,
                has_side_effects=True,
                vmem_limit_bytes=62 * 2**20,
            ),
        )(
            strain,
            bands.reshape(points // n, n),
            damaged.reshape(1, n),
            owner.reshape(1, n),
            w1,
            w2,
            outw,
            scale,
            back,
        )

    both = ("sec", "dev")
    return jax.shard_map(
        per_device,
        mesh=mesh,
        in_specs=(
            P(both, None),
            P(both),
            P(both),
            P(both, None),
            P(both, None),
            P(None, "sec"),
            P("sec", None),
            P(),
            P(),
        ),
        out_specs=P(both, None),
        check_vma=False,
    )
```

```python
import functools

import jax
import jax.numpy as jnp
from jax import lax
from jax.experimental import pallas as pl
from jax.experimental.pallas import tpu as pltpu
from jax.sharding import PartitionSpec as P

MESH = pl.DeviceIdType.MESH
BF = jnp.bfloat16
F32 = jnp.float32
CHUNKS = 4


def iota(shape, axis):
    return lax.broadcasted_iota(jnp.int32, shape, axis)


def mm(a, b):
    return jnp.dot(a, b, preferred_element_type=F32)


def hot(cond):
    return jnp.where(cond, 1.0, 0.0).astype(BF)


def half_silu(u):
    return u + u * jnp.tanh(u)


def wait_bytes(ref, sem):
    pltpu.make_async_copy(ref, ref, sem).wait()


def kernel(
    nx,
    nd,
    ne,
    strain_hbm,
    bands_ref,
    damaged_ref,
    owner_ref,
    w1_hbm,
    w2_hbm,
    outw_ref,
    scale_ref,
    back_ref,
    out_ref,
    strain_v,
    w1_v,
    w2_v,
    scale_v,
    scales_v,
    gather_v,
    dispatch_v,
    combine_v,
    feats_v,
    x0_v,
    x1_v,
    s0_v,
    z0_v,
    s1_v,
    a0_v,
    a1_v,
    xw_v,
    h_v,
    acc_v,
    m_v,
    r0_v,
    r1_v,
    t0_v,
    t1_v,
    y0_v,
    y1_v,
    local_sem,
    w1own_sem,
    w1send_sem,
    w1recv_sem,
    send_sem,
    recv_sem,
):
    x = lax.axis_index("sec")
    d = lax.axis_index("dev")
    barrier = pltpu.get_barrier_semaphore()
    n = 128
    ch = w1_v.shape[3]
    right, left = lax.rem(x + 1, nx), lax.rem(x + nx - 1, nx)

    def at_x(k):
        return lax.rem(x + k, nx)

    for k in range(1, nx):
        pl.semaphore_signal(barrier, inc=1, device_id=(at_x(k), d), device_id_type=MESH)

    z, e = d // ne, d % ne
    nz = nd // ne

    def at_z(k):
        return lax.rem(z + k, nz) * ne + e

    def at_e(k):
        return z * ne + lax.rem(e + k, ne)

    for k in range(1, nz):
        pl.semaphore_signal(barrier, inc=1, device_id=(x, at_z(k)), device_id_type=MESH)
    for k in range(1, ne):
        pl.semaphore_signal(barrier, inc=1, device_id=(x, at_e(k)), device_id_type=MESH)

    strain_copy = pltpu.make_async_copy(strain_hbm, strain_v, local_sem.at[0])
    strain_copy.start()
    w2_copy = pltpu.make_async_copy(w2_hbm, w2_v, local_sem.at[1])
    w2_copy.start()
    own_copies = []
    for c in range(CHUNKS):
        own = pltpu.make_async_copy(
            w1_hbm.at[:, pl.ds(c * ch, ch)], w1_v.at[c, 0], w1own_sem.at[c]
        )
        own.start()
        own_copies.append(own)

    eye = iota((n, n), 0) == iota((n, n), 1)
    ones = jnp.ones((n, n), BF)

    def spread(row):
        return mm(jnp.where(eye, row, 0.0).astype(BF), ones)

    damaged = damaged_ref[...]
    high = spread((damaged // n).astype(F32))
    low = spread((damaged % n).astype(F32))
    lane = iota((n, n), 1).astype(F32)
    on_low = low == lane
    band_part = jnp.zeros((n, n), F32)
    for b in range(strain_v.shape[0] // n):
        picked = jnp.logical_and(on_low, high == float(b))
        gather_v[:, b * n : (b + 1) * n] = hot(picked)
        band_part += jnp.where(picked, bands_ref[b : b + 1, :].astype(F32), 0.0)
    band_spread = mm(band_part.astype(BF), ones)
    band_row = jnp.sum(jnp.where(eye, band_spread, 0.0), axis=0, keepdims=True)
    owner_row = owner_ref[...].astype(F32)
    earlier = jnp.logical_and(
        spread(owner_row) == owner_row, iota((n, n), 0) < iota((n, n), 1)
    )
    rank = jnp.sum(jnp.where(earlier, 1.0, 0.0), axis=0, keepdims=True)
    target_row = 2.0 * owner_row + rank
    meta_at = iota((16, n), 0)
    x0_v[0, n : n + 16, :] = jnp.where(
        meta_at == 0, target_row, jnp.where(meta_at == 1, band_row, 0.0)
    ).astype(BF)
    strain_copy.wait()
    feats = mm(gather_v[...], strain_v[...])
    feats_v[...] = feats
    x0_v[0, 0:n, :] = feats.astype(BF)

    half = scale_ref[...] * 0.5
    term0 = half.astype(BF)
    rest = half - term0.astype(F32)
    term1 = rest.astype(BF)
    term2 = (rest - term1.astype(F32)).astype(BF)
    scale_v[0:16, :] = term0
    scale_v[16:32, :] = term1
    scale_v[32:48, :] = term2
    scale_v[48:128, :] = jnp.zeros((80, scale_v.shape[1]), BF)

    pl.semaphore_wait(barrier, nx - 1 + nz - 1 + ne - 1)

    def send_along_x(src_of, dst, sem):
        for k in range(1, nx):
            pltpu.make_async_remote_copy(
                src_ref=src_of(k),
                dst_ref=dst.at[(nx - k) % nx],
                send_sem=send_sem.at[sem],
                recv_sem=recv_sem.at[sem],
                device_id=(at_x(k), d),
                device_id_type=MESH,
            ).start()

    def send_all(src, dst, sem):
        @pl.loop(1, nd)
        def _(i):
            to = lax.rem(d + i, nd)
            pltpu.make_async_remote_copy(
                src_ref=src.at[to],
                dst_ref=dst.at[d],
                send_sem=send_sem.at[sem],
                recv_sem=recv_sem.at[sem],
                device_id=(x, to),
                device_id_type=MESH,
            ).start()

        dst[pl.ds(d, 1)] = src[pl.ds(d, 1)]

    send_along_x(lambda k: x0_v.at[0], x0_v, 0)

    def w1_copy(src, c, slot, to, sem):
        return pltpu.make_async_remote_copy(
            src_ref=src,
            dst_ref=w1_v.at[c, slot],
            send_sem=w1send_sem.at[sem, c],
            recv_sem=w1recv_sem.at[slot, c],
            device_id=(to, d),
            device_id_type=MESH,
        )

    w1_copies = {}
    to_right = range(CHUNKS)
    to_left = [(c + CHUNKS // 2) % CHUNKS for c in to_right]
    for c, e_c in zip(to_right, to_left):
        w1_copies[3, c] = w1_copy(w1_hbm.at[:, pl.ds(c * ch, ch)], c, 3, right, 1)
        w1_copies[1, e_c] = w1_copy(w1_hbm.at[:, pl.ds(e_c * ch, ch)], e_c, 1, left, 0)
        w1_copies[3, c].start()
        w1_copies[1, e_c].start()

    def forward(i):
        c, e_c = to_right[i], to_left[i]
        w1_copies[3, c].wait_recv()
        w1_copies[2, c] = w1_copy(w1_v.at[c, 3], c, 2, right, 2)
        w1_copies[2, c].start()
        w1_copies[1, e_c].wait_recv()
        w1_copies[2, e_c] = w1_copy(w1_v.at[e_c, 1], e_c, 2, left, 2)
        w1_copies[2, e_c].start()

    rows = nd * 32
    wait_bytes(x0_v.at[pl.ds(1, nx - 1)], recv_sem.at[0])

    def slot_code(at):
        dest, owner_at = at // 32, (at // 8) % 4
        lister, slot = (at // 2) % 4, at % 2
        code = (lax.rem(x + owner_at, nx) * nd + dest) * 2 + slot
        return code, lister

    down, down_lister = slot_code(iota((rows, n), 0))
    along, along_lister = slot_code(iota((n, rows), 1))
    band_cols = []
    for j in range(nx):
        meta = x0_v[j, n : n + 16, :].astype(F32)
        target_j, band_j = meta[0:1, :], meta[1:2, :]
        dispatch_v[:, j * n : (j + 1) * n] = hot(
            jnp.where(down_lister == j, down, -1).astype(F32) == target_j
        )
        target_down = spread(target_j)
        for b in range(rows // n):
            cut = slice(b * n, (b + 1) * n)
            combine_v[j * n : (j + 1) * n, cut] = hot(
                jnp.where(along_lister[:, cut] == j, along[:, cut], -1).astype(F32)
                == target_down
            )
        band_cols.append(spread(band_j).astype(BF))
    bands_all = jnp.concatenate(band_cols, axis=0)

    def spread_rows(features):
        return mm(dispatch_v[...], features).astype(BF).reshape(nd, 32, n)

    sent = spread_rows(x0_v[:, 0:n, :].reshape(nx * n, n))
    s0_v[:, :, 0:32, :] = sent.reshape(nz, ne, 32, n)
    s0_v[:, :, 32:64, :] = spread_rows(bands_all).reshape(nz, ne, 32, n)
    for k in range(1, nz):
        pltpu.make_async_remote_copy(
            src_ref=s0_v.at[lax.rem(z + k, nz)],
            dst_ref=z0_v.at[z],
            send_sem=send_sem.at[1],
            recv_sem=recv_sem.at[1],
            device_id=(x, at_z(k)),
            device_id_type=MESH,
        ).start()
    z0_v[pl.ds(z, 1)] = s0_v[pl.ds(z, 1)]
    wait_bytes(z0_v.at[pl.ds(0, nz - 1)], recv_sem.at[1])
    for k in range(1, ne):
        pltpu.make_async_remote_copy(
            src_ref=z0_v.at[:, lax.rem(e + k, ne)],
            dst_ref=a0_v.at[:, e],
            send_sem=send_sem.at[8],
            recv_sem=recv_sem.at[8],
            device_id=(x, at_e(k)),
            device_id_type=MESH,
        ).start()
    a0_v[:, pl.ds(e, 1)] = z0_v[:, pl.ds(e, 1)]
    wait_bytes(a0_v.at[:, pl.ds(0, ne - 1)], recv_sem.at[8])
    for i in range(CHUNKS // 2):
        forward(i)

    pair_rows = nd * 16
    level = iota((pair_rows, n), 1)
    level_of = jnp.where(level < 48, level % 16, -1).astype(F32)
    for p in range(2):
        got = a0_v[:, :, 32 + 16 * p : 48 + 16 * p, :].reshape(pair_rows, n)
        picks = hot(got.astype(F32) == level_of)
        for c in range(CHUNKS):
            cols = slice(c * ch, (c + 1) * ch)
            scales_v[p, :, cols] = mm(picks, scale_v[:, cols])

    def widen(got, p):
        which = (iota((pair_rows, n), 0) // 8) % 2
        value = got[:, 16 * p : 16 * p + 16, :].reshape(pair_rows, n)
        zero = jnp.zeros_like(value)
        xw_v[p, :, 0:n] = jnp.where(which == 0, value, zero)
        xw_v[p, :, n : 2 * n] = jnp.where(which == 1, value, zero)

    def first(p, c):
        cols = slice(c * ch, (c + 1) * ch)
        layer = w1_v[c, 2 * p : 2 * p + 2].reshape(2 * n, ch)
        u = mm(xw_v[p], layer) * scales_v[p, :, cols]
        h_v[p * pair_rows : (p + 1) * pair_rows, cols] = half_silu(u).astype(BF)

    def second(row, count, ranges, start, end):
        @pl.loop(0, w2_v.shape[1] // 256)
        def _(t):
            cols = pl.ds(pl.multiple_of(t * 256, 256), 256)
            part = None
            for lo, hi in ranges:
                term = mm(h_v[row : row + count, lo:hi], w2_v[lo:hi, cols])
                part = term if part is None else part + term
            if not start:
                part += acc_v[0:count, cols]
            if end:
                m_v[row : row + count, cols] = half_silu(part * 0.5).astype(BF)
            else:
                acc_v[0:count, cols] = part

    def third(row, count):
        total = mm(m_v[row : row + count, :], outw_ref[...])
        return total.astype(BF).reshape(nd, 16, n)

    def give_back(r_v, t_v, y_v, sem):
        for p in range(2):
            r_v[:, 16 * p : 16 * p + 16, :] = third(p * pair_rows, pair_rows)
        send_all(r_v, t_v, sem)
        wait_bytes(t_v.at[pl.ds(0, nd - 1)], recv_sem.at[sem])
        points = mm(combine_v[...], t_v[...].reshape(rows, n))
        y_v[...] = points.astype(BF).reshape(nx, n, n)

    def sum_along_x(y_v, y_in, sem):
        send_along_x(lambda k: y_v.at[k], y_in, sem)
        wait_bytes(y_in.at[pl.ds(1, nx - 1)], recv_sem.at[sem])
        total = y_v[0].astype(F32)
        for k in range(1, nx):
            total += y_in[k].astype(F32)
        return total.astype(BF)

    for p in range(2):
        widen(a0_v[...].reshape(nd, 64, n), p)
    w2_copy.wait()
    for i in range(CHUNKS):
        c = to_left[i]
        own_copies[c].wait()
        if i >= CHUNKS // 2:
            w1_copies[1, c].wait_recv()
            w1_copies[3, to_right[i]].wait_recv()
        first(0, c)
    hid = w2_v.shape[0]
    second(0, pair_rows, [(0, hid)], True, True)
    for i in range(CHUNKS // 2):
        ranges = []
        for c in (to_right[i], to_left[i]):
            w1_copies[2, c].wait_recv()
            first(1, c)
            ranges.append((c * ch, (c + 1) * ch))
        second(pair_rows, pair_rows, ranges, i == 0, i == CHUNKS // 2 - 1)
    give_back(r0_v, t0_v, y0_v.at[0], 2)
    values = sum_along_x(y0_v.at[0], y0_v.at[1], 3)
    features = (feats_v[...] + mm(values, back_ref[...])).astype(BF)

    x1_v[0] = features
    send_along_x(lambda k: x1_v.at[0], x1_v, 4)
    wait_bytes(x1_v.at[pl.ds(1, nx - 1)], recv_sem.at[4])
    s1_v[...] = spread_rows(x1_v[...].reshape(nx * n, n))
    send_all(s1_v, a1_v, 5)
    wait_bytes(a1_v.at[pl.ds(0, nd - 1)], recv_sem.at[5])
    for p in range(2):
        widen(a1_v[...], p)
        for c in range(CHUNKS):
            first(p, c)
    second(0, rows, [(0, hid)], True, True)
    give_back(r1_v, t1_v, y1_v.at[0], 6)
    out_ref[...] = sum_along_x(y1_v.at[0], y1_v.at[1], 7)

    for copy in w1_copies.values():
        copy.wait_send()
    wait_bytes(x0_v.at[pl.ds(1, nx - 1)], send_sem.at[0])
    wait_bytes(z0_v.at[pl.ds(0, nz - 1)], send_sem.at[1])
    wait_bytes(a0_v.at[:, pl.ds(0, ne - 1)], send_sem.at[8])
    wait_bytes(t0_v.at[pl.ds(0, nd - 1)], send_sem.at[2])
    wait_bytes(y0_v.at[1, pl.ds(1, nx - 1)], send_sem.at[3])
    wait_bytes(x1_v.at[pl.ds(1, nx - 1)], send_sem.at[4])
    wait_bytes(a1_v.at[pl.ds(0, nd - 1)], send_sem.at[5])
    wait_bytes(t1_v.at[pl.ds(0, nd - 1)], send_sem.at[6])
    wait_bytes(y1_v.at[1, pl.ds(1, nx - 1)], send_sem.at[7])


def solution(mesh):
    nx, nd = mesh.shape["sec"], mesh.shape["dev"]
    ne = 8

    def per_device(strain, bands, damaged, owner, w1, w2, outw, scale, back):
        n, hid = w1.shape
        points = strain.shape[0]
        mid = w2.shape[1]
        rows = nd * 32
        vmem = pl.BlockSpec(memory_space=pltpu.VMEM)
        hbm = pl.BlockSpec(memory_space=pl.ANY)
        return pl.pallas_call(
            functools.partial(kernel, nx, nd, ne),
            out_shape=jax.ShapeDtypeStruct((n, outw.shape[1]), BF),
            in_specs=[hbm, vmem, vmem, vmem, hbm, hbm, vmem, vmem, vmem],
            out_specs=vmem,
            scratch_shapes=[
                pltpu.VMEM((points, n), BF),
                pltpu.VMEM((CHUNKS, nx, n, hid // CHUNKS), BF),
                pltpu.VMEM((hid, mid), BF),
                pltpu.VMEM((n, hid), BF),
                pltpu.VMEM((2, rows // 2, hid), F32),
                pltpu.VMEM((n, points), BF),
                pltpu.VMEM((rows, nx * n), BF),
                pltpu.VMEM((nx * n, rows), BF),
                pltpu.VMEM((n, n), F32),
                pltpu.VMEM((nx, n + 16, n), BF),
                pltpu.VMEM((nx, n, n), BF),
                pltpu.VMEM((nd // ne, ne, 64, n), BF),
                pltpu.VMEM((nd // ne, ne, 64, n), BF),
                pltpu.VMEM((nd, 32, n), BF),
                pltpu.VMEM((nd // ne, ne, 64, n), BF),
                pltpu.VMEM((nd, 32, n), BF),
                pltpu.VMEM((2, rows // 2, 2 * n), BF),
                pltpu.VMEM((rows, hid), BF),
                pltpu.VMEM((rows // 2, mid), F32),
                pltpu.VMEM((rows, mid), BF),
                pltpu.VMEM((nd, 32, n), BF),
                pltpu.VMEM((nd, 32, n), BF),
                pltpu.VMEM((nd, 32, n), BF),
                pltpu.VMEM((nd, 32, n), BF),
                pltpu.VMEM((2, nx, n, n), BF),
                pltpu.VMEM((2, nx, n, n), BF),
                pltpu.SemaphoreType.DMA((2,)),
                pltpu.SemaphoreType.DMA((CHUNKS,)),
                pltpu.SemaphoreType.DMA((3, CHUNKS)),
                pltpu.SemaphoreType.DMA((nx, CHUNKS)),
                pltpu.SemaphoreType.DMA((9,)),
                pltpu.SemaphoreType.DMA((9,)),
            ],
            compiler_params=pltpu.CompilerParams(
                collective_id=0,
                has_side_effects=True,
                vmem_limit_bytes=62 * 2**20,
            ),
        )(
            strain,
            bands.reshape(points // n, n),
            damaged.reshape(1, n),
            owner.reshape(1, n),
            w1,
            w2,
            outw,
            scale,
            back,
        )

    both = ("sec", "dev")
    return jax.shard_map(
        per_device,
        mesh=mesh,
        in_specs=(
            P(both, None),
            P(both),
            P(both),
            P(both, None),
            P(both, None),
            P(None, "sec"),
            P("sec", None),
            P(),
            P(),
        ),
        out_specs=P(both, None),
        check_vma=False,
    )
```

```python
import functools

import jax
import jax.numpy as jnp
from jax import lax
from jax.experimental import pallas as pl
from jax.experimental.pallas import tpu as pltpu
from jax.sharding import PartitionSpec as P

MESH = pl.DeviceIdType.MESH
BF = jnp.bfloat16
F32 = jnp.float32
CHUNKS = 8
MSG = BF


def iota(shape, axis):
    return lax.broadcasted_iota(jnp.int32, shape, axis)


def mm(a, b):
    return jnp.dot(a, b, preferred_element_type=F32)


def hot(cond):
    return jnp.where(cond, 1.0, 0.0).astype(BF)


def half_silu(u):
    return u + u * jnp.tanh(u)


def wait_bytes(ref, sem):
    pltpu.make_async_copy(ref, ref, sem).wait()


def kernel(
    nx,
    nd,
    ne,
    strain_hbm,
    bands_ref,
    damaged_ref,
    owner_ref,
    w1_hbm,
    w2_hbm,
    outw_ref,
    scale_ref,
    back_ref,
    out_ref,
    strain_v,
    w1_v,
    w2_v,
    scale_v,
    scales_v,
    gather_v,
    dispatch_v,
    combine_v,
    direct_v,
    feats_v,
    x0_v,
    s0_v,
    z0_v,
    q1_v,
    a0_v,
    u1_v,
    xw_v,
    h_v,
    acc_v,
    m_v,
    r0_v,
    r1_v,
    t0_v,
    t1_v,
    local_sem,
    w1own_sem,
    w1send_sem,
    w1recv_sem,
    send_sem,
    recv_sem,
):
    x = lax.axis_index("sec")
    d = lax.axis_index("dev")
    barrier = pltpu.get_barrier_semaphore()
    n = 128
    ch = w1_v.shape[3]
    right, left = lax.rem(x + 1, nx), lax.rem(x + nx - 1, nx)

    def at_x(k):
        return lax.rem(x + k, nx)

    for k in range(1, nx):
        pl.semaphore_signal(barrier, inc=1, device_id=(at_x(k), d), device_id_type=MESH)

    z, e = d // ne, d % ne
    nz = nd // ne

    def at_z(k):
        return lax.rem(z + k, nz) * ne + e

    def at_e(k):
        return z * ne + lax.rem(e + k, ne)

    for k in range(1, nz):
        pl.semaphore_signal(barrier, inc=1, device_id=(x, at_z(k)), device_id_type=MESH)
    for k in range(1, ne):
        pl.semaphore_signal(barrier, inc=1, device_id=(x, at_e(k)), device_id_type=MESH)

    strain_copy = pltpu.make_async_copy(strain_hbm, strain_v, local_sem.at[0])
    strain_copy.start()
    w2_copy = pltpu.make_async_copy(w2_hbm, w2_v, local_sem.at[1])
    w2_copy.start()
    own_copies = []
    for c in range(CHUNKS):
        own = pltpu.make_async_copy(
            w1_hbm.at[:, pl.ds(c * ch, ch)], w1_v.at[c, 0], w1own_sem.at[c]
        )
        own.start()
        own_copies.append(own)

    eye = iota((n, n), 0) == iota((n, n), 1)
    ones = jnp.ones((n, n), BF)

    def spread(row):
        return mm(jnp.where(eye, row, 0.0).astype(BF), ones)

    damaged = damaged_ref[...]
    high = spread((damaged // n).astype(F32))
    low = spread((damaged % n).astype(F32))
    lane = iota((n, n), 1).astype(F32)
    on_low = low == lane
    band_part = jnp.zeros((n, n), F32)
    for b in range(strain_v.shape[0] // n):
        picked = jnp.logical_and(on_low, high == float(b))
        gather_v[:, b * n : (b + 1) * n] = hot(picked)
        band_part += jnp.where(picked, bands_ref[b : b + 1, :].astype(F32), 0.0)
    band_spread = mm(band_part.astype(BF), ones)
    band_row = jnp.sum(jnp.where(eye, band_spread, 0.0), axis=0, keepdims=True)
    owner_row = owner_ref[...].astype(F32)
    earlier = jnp.logical_and(
        spread(owner_row) == owner_row, iota((n, n), 0) < iota((n, n), 1)
    )
    rank = jnp.sum(jnp.where(earlier, 1.0, 0.0), axis=0, keepdims=True)
    target_row = 2.0 * owner_row + rank
    meta_at = iota((16, n), 0)
    x0_v[0, n : n + 16, :] = jnp.where(
        meta_at == 0, target_row, jnp.where(meta_at == 1, band_row, 0.0)
    ).astype(BF)
    strain_copy.wait()
    feats = mm(gather_v[...], strain_v[...])
    feats_v[...] = feats
    x0_v[0, 0:n, :] = feats.astype(BF)

    half = scale_ref[...] * 0.5
    term0 = half.astype(BF)
    rest = half - term0.astype(F32)
    term1 = rest.astype(BF)
    term2 = (rest - term1.astype(F32)).astype(BF)
    scale_v[0:16, :] = term0
    scale_v[16:32, :] = term1
    scale_v[32:48, :] = term2
    scale_v[48:128, :] = jnp.zeros((80, scale_v.shape[1]), BF)

    pl.semaphore_wait(barrier, nx - 1 + nz - 1 + ne - 1)

    def send_along_x(src_of, dst, sem):
        for k in range(1, nx):
            pltpu.make_async_remote_copy(
                src_ref=src_of(k),
                dst_ref=dst.at[(nx - k) % nx],
                send_sem=send_sem.at[sem],
                recv_sem=recv_sem.at[sem],
                device_id=(at_x(k), d),
                device_id_type=MESH,
            ).start()

    def send_direct(src, dst, sem):
        @pl.loop(1, nx * nd)
        def _(i):
            to = lax.rem(x * nd + d + i, nx * nd)
            to_x, to_d = to // nd, to % nd
            off = lax.rem(to_x - x + nx, nx)
            pltpu.make_async_remote_copy(
                src_ref=src.at[to_d * nx + off],
                dst_ref=dst.at[d * nx + lax.rem(nx - off, nx)],
                send_sem=send_sem.at[sem],
                recv_sem=recv_sem.at[sem],
                device_id=(to_x, to_d),
                device_id_type=MESH,
            ).start()

        dst[pl.ds(d * nx, 1)] = src[pl.ds(d * nx, 1)]
        wait_bytes(dst.at[pl.ds(0, nx * nd - 1)], recv_sem.at[sem])

    send_along_x(lambda k: x0_v.at[0], x0_v, 0)

    def w1_copy(src, c, slot, to, sem):
        return pltpu.make_async_remote_copy(
            src_ref=src,
            dst_ref=w1_v.at[c, slot],
            send_sem=w1send_sem.at[sem, c],
            recv_sem=w1recv_sem.at[slot, c],
            device_id=(to, d),
            device_id_type=MESH,
        )

    w1_copies = {}
    to_right = range(CHUNKS)
    to_left = [(c + CHUNKS // 2) % CHUNKS for c in to_right]
    for c, e_c in zip(to_right, to_left):
        w1_copies[3, c] = w1_copy(w1_hbm.at[:, pl.ds(c * ch, ch)], c, 3, right, 1)
        w1_copies[1, e_c] = w1_copy(w1_hbm.at[:, pl.ds(e_c * ch, ch)], e_c, 1, left, 0)
        w1_copies[3, c].start()
        w1_copies[1, e_c].start()

    def forward(i):
        c, e_c = to_right[i], to_left[i]
        w1_copies[3, c].wait_recv()
        w1_copies[2, c] = w1_copy(w1_v.at[c, 3], c, 2, right, 2)
        w1_copies[2, c].start()
        w1_copies[1, e_c].wait_recv()
        w1_copies[2, e_c] = w1_copy(w1_v.at[e_c, 1], e_c, 2, left, 2)
        w1_copies[2, e_c].start()

    rows = nd * 32
    wait_bytes(x0_v.at[pl.ds(1, nx - 1)], recv_sem.at[0])

    def slot_code(dest, owner_at, slot):
        return (lax.rem(x + owner_at, nx) * nd + dest) * 2 + slot

    at = iota((rows, n), 0)
    down = slot_code(at // 32, (at // 16) % 2 * 2 + (at // 2) % 2, at % 2)
    down_lister = (at // 4) % 4
    band_cols = []
    for j in range(nx):
        meta = x0_v[j, n : n + 16, :].astype(F32)
        target_j, band_j = meta[0:1, :], meta[1:2, :]
        dispatch_v[:, j * n : (j + 1) * n] = hot(
            jnp.where(down_lister == j, down, -1).astype(F32) == target_j
        )
        band_cols.append(spread(band_j).astype(BF))
    bands_all = jnp.concatenate(band_cols, axis=0)

    def spread_rows(features):
        return mm(dispatch_v[...], features).astype(BF).reshape(nd, 32, n)

    sent = spread_rows(x0_v[:, 0:n, :].reshape(nx * n, n))
    s0_v[:, :, 0:32, :] = sent.reshape(nz, ne, 32, n)
    s0_v[:, :, 32:64, :] = spread_rows(bands_all).reshape(nz, ne, 32, n)
    for k in range(1, nz):
        pltpu.make_async_remote_copy(
            src_ref=s0_v.at[lax.rem(z + k, nz)],
            dst_ref=z0_v.at[z],
            send_sem=send_sem.at[1],
            recv_sem=recv_sem.at[1],
            device_id=(x, at_z(k)),
            device_id_type=MESH,
        ).start()
    z0_v[pl.ds(z, 1)] = s0_v[pl.ds(z, 1)]
    wait_bytes(z0_v.at[pl.ds(0, nz - 1)], recv_sem.at[1])
    for k in range(1, ne):
        pltpu.make_async_remote_copy(
            src_ref=z0_v.at[:, lax.rem(e + k, ne)],
            dst_ref=a0_v.at[:, e],
            send_sem=send_sem.at[5],
            recv_sem=recv_sem.at[5],
            device_id=(x, at_e(k)),
            device_id_type=MESH,
        ).start()
    a0_v[:, pl.ds(e, 1)] = z0_v[:, pl.ds(e, 1)]
    wait_bytes(a0_v.at[:, pl.ds(0, ne - 1)], recv_sem.at[5])
    direct_v[...] = hot(
        slot_code(at // 32, (at // 8) % 4 + (at // 2) % 4, at % 2).astype(F32)
        == target_row
    )
    at = iota((n, rows), 1)
    combine_v[...] = hot(
        slot_code(at // 32, (at // 8) % 4 + (at // 2) % 4, at % 2).astype(F32)
        == jnp.concatenate([spread(target_row)] * (rows // n), axis=1)
    )
    pair_rows = nd * 16
    forward(0)
    forward(1)
    level = iota((pair_rows, n), 1)
    level_of = jnp.where(level < 48, level % 16, -1).astype(F32)
    for p in range(2):
        got = a0_v[:, :, 32 + 16 * p : 48 + 16 * p, :].reshape(pair_rows, n)
        picks = hot(got.astype(F32) == level_of)
        for c in range(CHUNKS):
            cols = slice(c * ch, (c + 1) * ch)
            scales_v[p, :, cols] = mm(picks, scale_v[:, cols])
        forward(2 + p)

    def widen(value, p):
        which = (iota((pair_rows, n), 0) // 2) % 2
        zero = jnp.zeros_like(value)
        xw_v[p, :, 0:n] = jnp.where(which == 0, value, zero).astype(BF)
        xw_v[p, :, n : 2 * n] = jnp.where(which == 1, value, zero).astype(BF)

    low_half = iota((rows // 16, 8, n), 1) < 4

    def swap(one, two):
        first_of = jnp.where(low_half, one, pltpu.roll(two, 4, axis=1))
        second_of = jnp.where(low_half, pltpu.roll(one, 4, axis=1), two)
        return first_of, second_of

    def first(p, c):
        cols = slice(c * ch, (c + 1) * ch)
        layer = w1_v[c, 2 * p : 2 * p + 2].reshape(2 * n, ch)
        u = mm(xw_v[p], layer) * scales_v[p, :, cols]
        h_v[p * pair_rows : (p + 1) * pair_rows, cols] = half_silu(u).astype(BF)

    def second(row, count, ranges, start, end):
        @pl.loop(0, w2_v.shape[1] // 256)
        def _(t):
            cols = pl.ds(pl.multiple_of(t * 256, 256), 256)
            part = None
            for lo, hi in ranges:
                term = mm(h_v[row : row + count, lo:hi], w2_v[lo:hi, cols])
                part = term if part is None else part + term
            if not start:
                part += acc_v[0:count, cols]
            if end:
                m_v[row : row + count, cols] = half_silu(part * 0.5).astype(BF)
            else:
                acc_v[0:count, cols] = part

    def give_back(r_v, t_v, sem):
        parts = []
        for p in range(2):
            total = mm(m_v[p * pair_rows : (p + 1) * pair_rows, :], outw_ref[...])
            parts.append(total.reshape(rows // 16, 8, n))
        even, odd = swap(*parts)
        r_v[...] = jnp.stack([even, odd], axis=1).reshape(rows // 8, 8, n).astype(MSG)
        send_direct(r_v, t_v, sem)
        return mm(combine_v[...], t_v[...].reshape(rows, n).astype(BF)).astype(BF)

    for p in range(2):
        got = a0_v[:, :, 16 * p : 16 * p + 16, :]
        widen(got.reshape(pair_rows, n), p)
    w2_copy.wait()
    for i in range(CHUNKS):
        c = to_left[i]
        own_copies[c].wait()
        if i >= CHUNKS // 2:
            w1_copies[1, c].wait_recv()
            w1_copies[3, to_right[i]].wait_recv()
        first(0, c)
    hid = w2_v.shape[0]
    second(0, pair_rows, [(0, hid)], True, True)
    for i in range(CHUNKS // 2):
        ranges = []
        for c in (to_right[i], to_left[i]):
            w1_copies[2, c].wait_recv()
            first(1, c)
            ranges.append((c * ch, (c + 1) * ch))
        second(pair_rows, pair_rows, ranges, i == 0, i == CHUNKS // 2 - 1)
    values = give_back(r0_v, t0_v, 2)
    features = (feats_v[...] + mm(values, back_ref[...])).astype(BF)

    q1_v[...] = mm(direct_v[...], features).reshape(rows // 8, 8, n).astype(MSG)
    send_direct(q1_v, u1_v, 3)
    got = u1_v[...].astype(F32).reshape(rows // 16, 2, 8, n)
    for p, value in enumerate(swap(got[:, 0], got[:, 1])):
        widen(value.reshape(pair_rows, n), p)
        for c in range(CHUNKS):
            first(p, c)
    second(0, rows, [(0, hid)], True, True)
    out_ref[...] = give_back(r1_v, t1_v, 4)

    for copy in w1_copies.values():
        copy.wait_send()
    wait_bytes(x0_v.at[pl.ds(1, nx - 1)], send_sem.at[0])
    wait_bytes(z0_v.at[pl.ds(0, nz - 1)], send_sem.at[1])
    wait_bytes(a0_v.at[:, pl.ds(0, ne - 1)], send_sem.at[5])
    for dst, sem in ((t0_v, 2), (u1_v, 3), (t1_v, 4)):
        wait_bytes(dst.at[pl.ds(0, nx * nd - 1)], send_sem.at[sem])


def solution(mesh):
    nx, nd = mesh.shape["sec"], mesh.shape["dev"]
    ne = 8

    def per_device(strain, bands, damaged, owner, w1, w2, outw, scale, back):
        n, hid = w1.shape
        points = strain.shape[0]
        mid = w2.shape[1]
        rows = nd * 32
        vmem = pl.BlockSpec(memory_space=pltpu.VMEM)
        hbm = pl.BlockSpec(memory_space=pl.ANY)
        return pl.pallas_call(
            functools.partial(kernel, nx, nd, ne),
            out_shape=jax.ShapeDtypeStruct((n, outw.shape[1]), BF),
            in_specs=[hbm, vmem, vmem, vmem, hbm, hbm, vmem, vmem, vmem],
            out_specs=vmem,
            scratch_shapes=[
                pltpu.VMEM((points, n), BF),
                pltpu.VMEM((CHUNKS, nx, n, hid // CHUNKS), BF),
                pltpu.VMEM((hid, mid), BF),
                pltpu.VMEM((n, hid), BF),
                pltpu.VMEM((2, rows // 2, hid), F32),
                pltpu.VMEM((n, points), BF),
                pltpu.VMEM((rows, nx * n), BF),
                pltpu.VMEM((n, rows), BF),
                pltpu.VMEM((rows, n), BF),
                pltpu.VMEM((n, n), F32),
                pltpu.VMEM((nx, n + 16, n), BF),
                pltpu.VMEM((nd // ne, ne, 64, n), BF),
                pltpu.VMEM((nd // ne, ne, 64, n), BF),
                pltpu.VMEM((rows // 8, 8, n), MSG),
                pltpu.VMEM((nd // ne, ne, 64, n), BF),
                pltpu.VMEM((rows // 8, 8, n), MSG),
                pltpu.VMEM((2, rows // 2, 2 * n), BF),
                pltpu.VMEM((rows, hid), BF),
                pltpu.VMEM((rows // 2, mid), F32),
                pltpu.VMEM((rows, mid), BF),
                pltpu.VMEM((rows // 8, 8, n), MSG),
                pltpu.VMEM((rows // 8, 8, n), MSG),
                pltpu.VMEM((rows // 8, 8, n), MSG),
                pltpu.VMEM((rows // 8, 8, n), MSG),
                pltpu.SemaphoreType.DMA((2,)),
                pltpu.SemaphoreType.DMA((CHUNKS,)),
                pltpu.SemaphoreType.DMA((3, CHUNKS)),
                pltpu.SemaphoreType.DMA((nx, CHUNKS)),
                pltpu.SemaphoreType.DMA((6,)),
                pltpu.SemaphoreType.DMA((6,)),
            ],
            compiler_params=pltpu.CompilerParams(
                collective_id=0,
                has_side_effects=True,
                vmem_limit_bytes=62 * 2**20,
            ),
        )(
            strain,
            bands.reshape(points // n, n),
            damaged.reshape(1, n),
            owner.reshape(1, n),
            w1,
            w2,
            outw,
            scale,
            back,
        )

    both = ("sec", "dev")
    return jax.shard_map(
        per_device,
        mesh=mesh,
        in_specs=(
            P(both, None),
            P(both),
            P(both),
            P(both, None),
            P(both, None),
            P(None, "sec"),
            P("sec", None),
            P(),
            P(),
        ),
        out_specs=P(both, None),
        check_vma=False,
    )
```

```python
import functools

import jax
import jax.numpy as jnp
from jax import lax
from jax.experimental import pallas as pl
from jax.experimental.pallas import tpu as pltpu
from jax.sharding import PartitionSpec as P

MESH = pl.DeviceIdType.MESH
BF = jnp.bfloat16
F32 = jnp.float32
CHUNKS = 8
MSG = BF


def iota(shape, axis):
    return lax.broadcasted_iota(jnp.int32, shape, axis)


def mm(a, b):
    return jnp.dot(a, b, preferred_element_type=F32)


def hot(cond):
    return jnp.where(cond, 1.0, 0.0).astype(BF)


def half_silu(u):
    return u + u * jnp.tanh(u)


def wait_bytes(ref, sem):
    pltpu.make_async_copy(ref, ref, sem).wait()


def kernel(
    nx,
    nd,
    ne,
    strain_hbm,
    bands_ref,
    damaged_ref,
    owner_ref,
    w1_hbm,
    w2_hbm,
    outw_ref,
    scale_ref,
    back_ref,
    out_ref,
    strain_v,
    w1_v,
    w2_v,
    scale_v,
    scales_v,
    gather_v,
    dispatch_v,
    combine_v,
    direct_v,
    picks_v,
    held_v,
    feats_v,
    x0_v,
    s0_v,
    z0_v,
    q1_v,
    a0_v,
    u1_v,
    xw_v,
    h_v,
    acc_v,
    m_v,
    r0_v,
    r1_v,
    t0_v,
    t1_v,
    local_sem,
    w1own_sem,
    w1send_sem,
    w1recv_sem,
    send_sem,
    recv_sem,
):
    x = lax.axis_index("sec")
    d = lax.axis_index("dev")
    barrier = pltpu.get_barrier_semaphore()
    n = 128
    ch = w1_v.shape[3]
    right, left = lax.rem(x + 1, nx), lax.rem(x + nx - 1, nx)

    def at_x(k):
        return lax.rem(x + k, nx)

    for k in range(1, nx):
        pl.semaphore_signal(barrier, inc=1, device_id=(at_x(k), d), device_id_type=MESH)

    z, e = d // ne, d % ne
    nz = nd // ne

    def at_z(k):
        return lax.rem(z + k, nz) * ne + e

    def at_e(k):
        return z * ne + lax.rem(e + k, ne)

    for k in range(1, nz):
        pl.semaphore_signal(barrier, inc=1, device_id=(x, at_z(k)), device_id_type=MESH)
    for k in range(1, ne):
        pl.semaphore_signal(barrier, inc=1, device_id=(x, at_e(k)), device_id_type=MESH)

    strain_copy = pltpu.make_async_copy(strain_hbm, strain_v, local_sem.at[0])
    strain_copy.start()
    w2_copy = pltpu.make_async_copy(w2_hbm, w2_v, local_sem.at[1])
    w2_copy.start()
    own_copies = []
    for c in range(CHUNKS):
        own = pltpu.make_async_copy(
            w1_hbm.at[:, pl.ds(c * ch, ch)], w1_v.at[c, 0], w1own_sem.at[c]
        )
        own.start()
        own_copies.append(own)

    eye = iota((n, n), 0) == iota((n, n), 1)
    ones = jnp.ones((n, n), BF)

    def spread(row):
        return mm(jnp.where(eye, row, 0.0).astype(BF), ones)

    damaged = damaged_ref[...]
    high = spread((damaged // n).astype(F32))
    low = spread((damaged % n).astype(F32))
    lane = iota((n, n), 1).astype(F32)
    on_low = low == lane
    band_part = jnp.zeros((n, n), F32)
    for b in range(strain_v.shape[0] // n):
        picked = jnp.logical_and(on_low, high == float(b))
        gather_v[:, b * n : (b + 1) * n] = hot(picked)
        band_part += jnp.where(picked, bands_ref[b : b + 1, :].astype(F32), 0.0)
    band_spread = mm(band_part.astype(BF), ones)
    band_row = jnp.sum(jnp.where(eye, band_spread, 0.0), axis=0, keepdims=True)
    owner_row = owner_ref[...].astype(F32)
    earlier = jnp.logical_and(
        spread(owner_row) == owner_row, iota((n, n), 0) < iota((n, n), 1)
    )
    rank = jnp.sum(jnp.where(earlier, 1.0, 0.0), axis=0, keepdims=True)
    target_row = 2.0 * owner_row + rank
    meta_at = iota((16, n), 0)
    x0_v[0, n : n + 16, :] = jnp.where(
        meta_at == 0, target_row, jnp.where(meta_at == 1, band_row, 0.0)
    ).astype(BF)
    strain_copy.wait()
    feats = mm(gather_v[...], strain_v[...])
    feats_v[...] = feats
    x0_v[0, 0:n, :] = feats.astype(BF)

    half = scale_ref[...] * 0.5
    term0 = half.astype(BF)
    rest = half - term0.astype(F32)
    term1 = rest.astype(BF)
    term2 = (rest - term1.astype(F32)).astype(BF)
    scale_v[0:16, :] = term0
    scale_v[16:32, :] = term1
    scale_v[32:48, :] = term2
    scale_v[48:128, :] = jnp.zeros((80, scale_v.shape[1]), BF)

    pl.semaphore_wait(barrier, nx - 1 + nz - 1 + ne - 1)

    def send_along_x(src_of, dst, sem):
        for k in range(1, nx):
            pltpu.make_async_remote_copy(
                src_ref=src_of(k),
                dst_ref=dst.at[(nx - k) % nx],
                send_sem=send_sem.at[sem],
                recv_sem=recv_sem.at[sem],
                device_id=(at_x(k), d),
                device_id_type=MESH,
            ).start()

    def send_direct(src, dst, sem):
        def send_to(to_d, offs):
            for off in offs:
                pltpu.make_async_remote_copy(
                    src_ref=src.at[to_d * nx + off],
                    dst_ref=dst.at[d * nx + (nx - off) % nx],
                    send_sem=send_sem.at[sem],
                    recv_sem=recv_sem.at[sem],
                    device_id=(at_x(off), to_d),
                    device_id_type=MESH,
                ).start()

        far_first = sorted(range(nx), key=lambda k: -min(k, nx - k))

        @pl.loop(0, nd // 2)
        def _(i):
            send_to(lax.rem(d + nd // 2 + i, nd), far_first)

        @pl.loop(1, nd // 2)
        def _(i):
            send_to(lax.rem(d + i, nd), far_first)

        send_to(d, [k for k in far_first if k])
        dst[pl.ds(d * nx, 1)] = src[pl.ds(d * nx, 1)]
        wait_bytes(dst.at[pl.ds(0, nx * nd - 1)], recv_sem.at[sem])

    send_along_x(lambda k: x0_v.at[0], x0_v, 0)

    def w1_copy(src, c, slot, to, sem):
        return pltpu.make_async_remote_copy(
            src_ref=src,
            dst_ref=w1_v.at[c, slot],
            send_sem=w1send_sem.at[sem, c],
            recv_sem=w1recv_sem.at[slot, c],
            device_id=(to, d),
            device_id_type=MESH,
        )

    w1_copies = {}
    to_right = range(CHUNKS)
    to_left = [(c + CHUNKS // 2) % CHUNKS for c in to_right]
    for c, e_c in zip(to_right, to_left):
        w1_copies[3, c] = w1_copy(w1_hbm.at[:, pl.ds(c * ch, ch)], c, 3, right, 1)
        w1_copies[1, e_c] = w1_copy(w1_hbm.at[:, pl.ds(e_c * ch, ch)], e_c, 1, left, 0)
        w1_copies[3, c].start()
        w1_copies[1, e_c].start()

    def forward(i):
        c, e_c = to_right[i], to_left[i]
        w1_copies[3, c].wait_recv()
        w1_copies[2, c] = w1_copy(w1_v.at[c, 3], c, 2, right, 2)
        w1_copies[2, c].start()
        w1_copies[1, e_c].wait_recv()
        w1_copies[2, e_c] = w1_copy(w1_v.at[e_c, 1], e_c, 2, left, 2)
        w1_copies[2, e_c].start()

    rows = nd * 32
    wait_bytes(x0_v.at[pl.ds(1, nx - 1)], recv_sem.at[0])

    def slot_code(dest, owner_at, slot):
        return (lax.rem(x + owner_at, nx) * nd + dest) * 2 + slot

    at = iota((rows, n), 0)
    down = slot_code(at // 32, (at // 16) % 2 * 2 + (at // 2) % 2, at % 2)
    down_lister = (at // 4) % 4
    band_cols = []
    for j in range(nx):
        meta = x0_v[j, n : n + 16, :].astype(F32)
        target_j, band_j = meta[0:1, :], meta[1:2, :]
        dispatch_v[:, j * n : (j + 1) * n] = hot(
            jnp.where(down_lister == j, down, -1).astype(F32) == target_j
        )
        band_cols.append(spread(band_j).astype(BF))
    bands_all = jnp.concatenate(band_cols, axis=0)

    def spread_rows(features):
        return mm(dispatch_v[...], features).astype(BF).reshape(nd, 32, n)

    sent = spread_rows(x0_v[:, 0:n, :].reshape(nx * n, n))
    s0_v[:, :, 0:32, :] = sent.reshape(nz, ne, 32, n)
    s0_v[:, :, 32:64, :] = spread_rows(bands_all).reshape(nz, ne, 32, n)
    for k in range(1, nz):
        pltpu.make_async_remote_copy(
            src_ref=s0_v.at[lax.rem(z + k, nz)],
            dst_ref=z0_v.at[z],
            send_sem=send_sem.at[1],
            recv_sem=recv_sem.at[1],
            device_id=(x, at_z(k)),
            device_id_type=MESH,
        ).start()
    direct_v[...] = hot(
        slot_code(at // 32, (at // 8) % 4 + (at // 2) % 4, at % 2).astype(F32)
        == target_row
    )
    at = iota((n, rows), 1)
    combine_v[...] = hot(
        slot_code(at // 32, (at // 8) % 4 + (at // 2) % 4, at % 2).astype(F32)
        == jnp.concatenate([spread(target_row)] * (rows // n), axis=1)
    )
    z0_v[pl.ds(z, 1)] = s0_v[pl.ds(z, 1)]
    wait_bytes(z0_v.at[pl.ds(0, nz - 1)], recv_sem.at[1])
    for k in range(1, ne):
        pltpu.make_async_remote_copy(
            src_ref=z0_v.at[:, lax.rem(e + k, ne)],
            dst_ref=a0_v.at[:, e],
            send_sem=send_sem.at[5],
            recv_sem=recv_sem.at[5],
            device_id=(x, at_e(k)),
            device_id_type=MESH,
        ).start()
    a0_v[:, pl.ds(e, 1)] = z0_v[:, pl.ds(e, 1)]
    wait_bytes(a0_v.at[:, pl.ds(0, ne - 1)], recv_sem.at[5])
    pair_rows = nd * 16
    level = iota((pair_rows, n), 1)
    level_of = jnp.where(level < 48, level % 16, -1).astype(F32)
    for p in range(2):
        got = a0_v[:, :, 32 + 16 * p : 48 + 16 * p, :].reshape(pair_rows, n)
        picks_v[p] = hot(got.astype(F32) == level_of)

    def widen(value, p):
        which = (iota((pair_rows, n), 0) // 2) % 2
        zero = jnp.zeros_like(value)
        xw_v[p, :, 0:n] = jnp.where(which == 0, value, zero).astype(BF)
        xw_v[p, :, n : 2 * n] = jnp.where(which == 1, value, zero).astype(BF)

    low_half = iota((rows // 16, 8, n), 1) < 4

    def swap(one, two):
        first_of = jnp.where(low_half, one, pltpu.roll(two, 4, axis=1))
        second_of = jnp.where(low_half, pltpu.roll(one, 4, axis=1), two)
        return first_of, second_of

    def first(p, c, pick=False):
        cols = slice(c * ch, (c + 1) * ch)
        layer = w1_v[c, 2 * p : 2 * p + 2].reshape(2 * n, ch)
        if pick:
            scales = mm(picks_v[p], scale_v[:, cols])
            scales_v[p, :, cols] = scales
        else:
            scales = scales_v[p, :, cols]
        u = mm(xw_v[p], layer) * scales
        h_v[p * pair_rows : (p + 1) * pair_rows, cols] = half_silu(u).astype(BF)

    def second(row, count, ranges, start, end):
        @pl.loop(0, w2_v.shape[1] // 512)
        def _(t):
            cols = pl.ds(pl.multiple_of(t * 512, 512), 512)
            part = None
            for lo, hi in ranges:
                term = mm(h_v[row : row + count, lo:hi], w2_v[lo:hi, cols])
                part = term if part is None else part + term
            if not start:
                part += acc_v[0:count, cols]
            if end:
                m_v[row : row + count, cols] = half_silu(part * 0.5).astype(BF)
            else:
                acc_v[0:count, cols] = part

    def third(p):
        total = mm(m_v[p * pair_rows : (p + 1) * pair_rows, :], outw_ref[...])
        return total.reshape(rows // 16, 8, n)

    def give_back(parts, r_v, t_v, sem):
        even, odd = swap(*parts)
        r_v[...] = jnp.stack([even, odd], axis=1).reshape(rows // 8, 8, n).astype(MSG)
        send_direct(r_v, t_v, sem)
        return mm(combine_v[...], t_v[...].reshape(rows, n).astype(BF)).astype(BF)

    for p in range(2):
        got = a0_v[:, :, 16 * p : 16 * p + 16, :]
        widen(got.reshape(pair_rows, n), p)
    w2_copy.wait()
    hid = w2_v.shape[0]
    for own in own_copies:
        own.wait()

    def span(chunks):
        return [(c * ch, (c + 1) * ch) for c in chunks]

    half = CHUNKS // 2
    for i in range(half):
        forward(i)
        first(0, to_left[i], True)
    second(0, pair_rows, [(hid // 2, hid)], True, False)
    for i in range(half, CHUNKS):
        w1_copies[1, to_left[i]].wait_recv()
        first(0, to_left[i], True)
    second(0, pair_rows, [(0, hid // 2)], False, True)
    held_v[...] = third(0)
    for i in range(half, CHUNKS):
        w1_copies[3, to_right[i]].wait_recv()
    for i in range(half):
        chunks = to_right[i], to_left[i]
        for c in chunks:
            w1_copies[2, c].wait_recv()
            first(1, c, True)
        second(pair_rows, pair_rows, span(chunks), i == 0, i == half - 1)
    values = give_back((held_v[...], third(1)), r0_v, t0_v, 2)
    features = (feats_v[...] + mm(values, back_ref[...])).astype(BF)

    q1_v[...] = mm(direct_v[...], features).reshape(rows // 8, 8, n).astype(MSG)
    send_direct(q1_v, u1_v, 3)
    got = u1_v[...].astype(F32).reshape(rows // 16, 2, 8, n)
    for p, value in enumerate(swap(got[:, 0], got[:, 1])):
        widen(value.reshape(pair_rows, n), p)
        for c in range(CHUNKS):
            first(p, c)
    second(0, rows, [(0, hid)], True, True)
    out_ref[...] = give_back((third(0), third(1)), r1_v, t1_v, 4)

    for copy in w1_copies.values():
        copy.wait_send()
    wait_bytes(x0_v.at[pl.ds(1, nx - 1)], send_sem.at[0])
    wait_bytes(z0_v.at[pl.ds(0, nz - 1)], send_sem.at[1])
    wait_bytes(a0_v.at[:, pl.ds(0, ne - 1)], send_sem.at[5])
    for dst, sem in ((t0_v, 2), (u1_v, 3), (t1_v, 4)):
        wait_bytes(dst.at[pl.ds(0, nx * nd - 1)], send_sem.at[sem])


def solution(mesh):
    nx, nd = mesh.shape["sec"], mesh.shape["dev"]
    ne = 8

    def per_device(strain, bands, damaged, owner, w1, w2, outw, scale, back):
        n, hid = w1.shape
        points = strain.shape[0]
        mid = w2.shape[1]
        rows = nd * 32
        vmem = pl.BlockSpec(memory_space=pltpu.VMEM)
        hbm = pl.BlockSpec(memory_space=pl.ANY)
        return pl.pallas_call(
            functools.partial(kernel, nx, nd, ne),
            out_shape=jax.ShapeDtypeStruct((n, outw.shape[1]), BF),
            in_specs=[hbm, vmem, vmem, vmem, hbm, hbm, vmem, vmem, vmem],
            out_specs=vmem,
            scratch_shapes=[
                pltpu.VMEM((points, n), BF),
                pltpu.VMEM((CHUNKS, nx, n, hid // CHUNKS), BF),
                pltpu.VMEM((hid, mid), BF),
                pltpu.VMEM((n, hid), BF),
                pltpu.VMEM((2, rows // 2, hid), F32),
                pltpu.VMEM((n, points), BF),
                pltpu.VMEM((rows, nx * n), BF),
                pltpu.VMEM((n, rows), BF),
                pltpu.VMEM((rows, n), BF),
                pltpu.VMEM((2, rows // 2, n), BF),
                pltpu.VMEM((rows // 16, 8, n), F32),
                pltpu.VMEM((n, n), F32),
                pltpu.VMEM((nx, n + 16, n), BF),
                pltpu.VMEM((nd // ne, ne, 64, n), BF),
                pltpu.VMEM((nd // ne, ne, 64, n), BF),
                pltpu.VMEM((rows // 8, 8, n), MSG),
                pltpu.VMEM((nd // ne, ne, 64, n), BF),
                pltpu.VMEM((rows // 8, 8, n), MSG),
                pltpu.VMEM((2, rows // 2, 2 * n), BF),
                pltpu.VMEM((rows, hid), BF),
                pltpu.VMEM((rows // 2, mid), F32),
                pltpu.VMEM((rows, mid), BF),
                pltpu.VMEM((rows // 8, 8, n), MSG),
                pltpu.VMEM((rows // 8, 8, n), MSG),
                pltpu.VMEM((rows // 8, 8, n), MSG),
                pltpu.VMEM((rows // 8, 8, n), MSG),
                pltpu.SemaphoreType.DMA((2,)),
                pltpu.SemaphoreType.DMA((CHUNKS,)),
                pltpu.SemaphoreType.DMA((3, CHUNKS)),
                pltpu.SemaphoreType.DMA((nx, CHUNKS)),
                pltpu.SemaphoreType.DMA((6,)),
                pltpu.SemaphoreType.DMA((6,)),
            ],
            compiler_params=pltpu.CompilerParams(
                collective_id=0,
                has_side_effects=True,
                vmem_limit_bytes=62 * 2**20,
            ),
        )(
            strain,
            bands.reshape(points // n, n),
            damaged.reshape(1, n),
            owner.reshape(1, n),
            w1,
            w2,
            outw,
            scale,
            back,
        )

    both = ("sec", "dev")
    return jax.shard_map(
        per_device,
        mesh=mesh,
        in_specs=(
            P(both, None),
            P(both),
            P(both),
            P(both, None),
            P(both, None),
            P(None, "sec"),
            P("sec", None),
            P(),
            P(),
        ),
        out_specs=P(both, None),
        check_vma=False,
    )
```

```python
import functools

import jax
import jax.numpy as jnp
from jax import lax
from jax.experimental import pallas as pl
from jax.experimental.pallas import tpu as pltpu
from jax.sharding import PartitionSpec as P

MESH = pl.DeviceIdType.MESH
BF = jnp.bfloat16
F32 = jnp.float32
CHUNKS = 8
MSG = BF


def iota(shape, axis):
    return lax.broadcasted_iota(jnp.int32, shape, axis)


def mm(a, b):
    return jnp.dot(a, b, preferred_element_type=F32)


def hot(cond):
    return jnp.where(cond, 1.0, 0.0).astype(BF)


def half_silu(u):
    return u + u * jnp.tanh(u)


def wait_bytes(ref, sem):
    pltpu.make_async_copy(ref, ref, sem).wait()


def kernel(
    nx,
    nd,
    ne,
    strain_hbm,
    bands_hbm,
    damaged_hbm,
    owner_hbm,
    w1_hbm,
    w2_hbm,
    outw_hbm,
    scale_hbm,
    back_hbm,
    out_ref,
    bands_ref,
    damaged_ref,
    owner_ref,
    outw_ref,
    scale_ref,
    back_ref,
    strain_v,
    w1_v,
    w2_v,
    scale_v,
    scales_v,
    gather_v,
    dispatch_v,
    combine_v,
    direct_v,
    picks_v,
    held_v,
    feats_v,
    x0_v,
    s0_v,
    z0_v,
    q1_v,
    a0_v,
    u1_v,
    xw_v,
    h_v,
    acc_v,
    m_v,
    r0_v,
    r1_v,
    t0_v,
    t1_v,
    local_sem,
    w1own_sem,
    w1send_sem,
    w1recv_sem,
    send_sem,
    recv_sem,
):
    x = lax.axis_index("sec")
    d = lax.axis_index("dev")
    barrier = pltpu.get_barrier_semaphore()
    n = 128
    ch = w1_v.shape[3]
    right, left = lax.rem(x + 1, nx), lax.rem(x + nx - 1, nx)

    def at_x(k):
        return lax.rem(x + k, nx)

    for k in range(1, nx):
        pl.semaphore_signal(barrier, inc=1, device_id=(at_x(k), d), device_id_type=MESH)

    z, e = d // ne, d % ne
    nz = nd // ne

    def at_z(k):
        return lax.rem(z + k, nz) * ne + e

    def at_e(k):
        return z * ne + lax.rem(e + k, ne)

    for k in range(1, nz):
        pl.semaphore_signal(barrier, inc=1, device_id=(x, at_z(k)), device_id_type=MESH)
    for k in range(1, ne):
        pl.semaphore_signal(barrier, inc=1, device_id=(x, at_e(k)), device_id_type=MESH)

    small = []
    for i, (src, dst) in enumerate(
        (
            (damaged_hbm, damaged_ref),
            (bands_hbm, bands_ref),
            (owner_hbm, owner_ref),
            (scale_hbm, scale_ref),
            (outw_hbm, outw_ref),
            (back_hbm, back_ref),
        )
    ):
        small.append(pltpu.make_async_copy(src, dst, local_sem.at[2 + i]))
        small[i].start()
    strain_copy = pltpu.make_async_copy(strain_hbm, strain_v, local_sem.at[0])
    strain_copy.start()
    w2_copy = pltpu.make_async_copy(w2_hbm, w2_v, local_sem.at[1])
    w2_copy.start()
    own_copies = []
    for c in range(CHUNKS):
        own = pltpu.make_async_copy(
            w1_hbm.at[:, pl.ds(c * ch, ch)], w1_v.at[c, 0], w1own_sem.at[c]
        )
        own.start()
        own_copies.append(own)

    eye = iota((n, n), 0) == iota((n, n), 1)
    ones = jnp.ones((n, n), BF)

    def spread(row):
        return mm(jnp.where(eye, row, 0.0).astype(BF), ones)

    for copy in small[:3]:
        copy.wait()
    damaged = damaged_ref[...]
    high = spread((damaged // n).astype(F32))
    low = spread((damaged % n).astype(F32))
    lane = iota((n, n), 1).astype(F32)
    on_low = low == lane
    band_part = jnp.zeros((n, n), F32)
    for b in range(strain_v.shape[0] // n):
        picked = jnp.logical_and(on_low, high == float(b))
        gather_v[:, b * n : (b + 1) * n] = hot(picked)
        band_part += jnp.where(picked, bands_ref[b : b + 1, :].astype(F32), 0.0)
    band_spread = mm(band_part.astype(BF), ones)
    band_row = jnp.sum(jnp.where(eye, band_spread, 0.0), axis=0, keepdims=True)
    owner_row = owner_ref[...].astype(F32)
    earlier = jnp.logical_and(
        spread(owner_row) == owner_row, iota((n, n), 0) < iota((n, n), 1)
    )
    rank = jnp.sum(jnp.where(earlier, 1.0, 0.0), axis=0, keepdims=True)
    target_row = 2.0 * owner_row + rank
    meta_at = iota((16, n), 0)
    x0_v[0, n : n + 16, :] = jnp.where(
        meta_at == 0, target_row, jnp.where(meta_at == 1, band_row, 0.0)
    ).astype(BF)
    strain_copy.wait()
    feats = mm(gather_v[...], strain_v[...])
    feats_v[...] = feats
    x0_v[0, 0:n, :] = feats.astype(BF)

    for copy in small[3:]:
        copy.wait()
    half = scale_ref[...] * 0.5
    term0 = half.astype(BF)
    rest = half - term0.astype(F32)
    term1 = rest.astype(BF)
    term2 = (rest - term1.astype(F32)).astype(BF)
    scale_v[0:16, :] = term0
    scale_v[16:32, :] = term1
    scale_v[32:48, :] = term2
    scale_v[48:128, :] = jnp.zeros((80, scale_v.shape[1]), BF)

    pl.semaphore_wait(barrier, nx - 1 + nz - 1 + ne - 1)

    def send_along_x(src_of, dst, sem):
        for k in range(1, nx):
            pltpu.make_async_remote_copy(
                src_ref=src_of(k),
                dst_ref=dst.at[(nx - k) % nx],
                send_sem=send_sem.at[sem],
                recv_sem=recv_sem.at[sem],
                device_id=(at_x(k), d),
                device_id_type=MESH,
            ).start()

    def send_direct(src, dst, sem):
        def send_to(to_d, offs):
            for off in offs:
                pltpu.make_async_remote_copy(
                    src_ref=src.at[to_d * nx + off],
                    dst_ref=dst.at[d * nx + (nx - off) % nx],
                    send_sem=send_sem.at[sem],
                    recv_sem=recv_sem.at[sem],
                    device_id=(at_x(off), to_d),
                    device_id_type=MESH,
                ).start()

        far_first = sorted(range(nx), key=lambda k: -min(k, nx - k))

        @pl.loop(0, nd // 2)
        def _(i):
            send_to(lax.rem(d + nd // 2 + i, nd), far_first)

        @pl.loop(1, nd // 2)
        def _(i):
            send_to(lax.rem(d + i, nd), far_first)

        send_to(d, [k for k in far_first if k])
        dst[pl.ds(d * nx, 1)] = src[pl.ds(d * nx, 1)]
        wait_bytes(dst.at[pl.ds(0, nx * nd - 1)], recv_sem.at[sem])

    send_along_x(lambda k: x0_v.at[0], x0_v, 0)

    def w1_copy(src, c, slot, to, sem):
        return pltpu.make_async_remote_copy(
            src_ref=src,
            dst_ref=w1_v.at[c, slot],
            send_sem=w1send_sem.at[sem, c],
            recv_sem=w1recv_sem.at[slot, c],
            device_id=(to, d),
            device_id_type=MESH,
        )

    w1_copies = {}
    to_right = range(CHUNKS)
    to_left = [(c + CHUNKS // 2) % CHUNKS for c in to_right]
    for c, e_c in zip(to_right, to_left):
        w1_copies[3, c] = w1_copy(w1_hbm.at[:, pl.ds(c * ch, ch)], c, 3, right, 1)
        w1_copies[1, e_c] = w1_copy(w1_hbm.at[:, pl.ds(e_c * ch, ch)], e_c, 1, left, 0)
        w1_copies[3, c].start()
        w1_copies[1, e_c].start()

    def forward(i):
        c, e_c = to_right[i], to_left[i]
        w1_copies[3, c].wait_recv()
        w1_copies[2, c] = w1_copy(w1_v.at[c, 3], c, 2, right, 2)
        w1_copies[2, c].start()
        w1_copies[1, e_c].wait_recv()
        w1_copies[2, e_c] = w1_copy(w1_v.at[e_c, 1], e_c, 2, left, 2)
        w1_copies[2, e_c].start()

    rows = nd * 32
    wait_bytes(x0_v.at[pl.ds(1, nx - 1)], recv_sem.at[0])

    def slot_code(dest, owner_at, slot):
        return (lax.rem(x + owner_at, nx) * nd + dest) * 2 + slot

    at = iota((rows, n), 0)
    down = slot_code(at // 32, (at // 16) % 2 * 2 + (at // 2) % 2, at % 2)
    down_lister = (at // 4) % 4
    band_cols = []
    for j in range(nx):
        meta = x0_v[j, n : n + 16, :].astype(F32)
        target_j, band_j = meta[0:1, :], meta[1:2, :]
        dispatch_v[:, j * n : (j + 1) * n] = hot(
            jnp.where(down_lister == j, down, -1).astype(F32) == target_j
        )
        band_cols.append(spread(band_j).astype(BF))
    bands_all = jnp.concatenate(band_cols, axis=0)

    def spread_rows(features):
        return mm(dispatch_v[...], features).astype(BF).reshape(nd, 32, n)

    sent = spread_rows(x0_v[:, 0:n, :].reshape(nx * n, n))
    s0_v[:, :, 0:32, :] = sent.reshape(nz, ne, 32, n)
    s0_v[:, :, 32:64, :] = spread_rows(bands_all).reshape(nz, ne, 32, n)
    for k in range(1, nz):
        pltpu.make_async_remote_copy(
            src_ref=s0_v.at[lax.rem(z + k, nz)],
            dst_ref=z0_v.at[z],
            send_sem=send_sem.at[1],
            recv_sem=recv_sem.at[1],
            device_id=(x, at_z(k)),
            device_id_type=MESH,
        ).start()
    direct_v[...] = hot(
        slot_code(at // 32, (at // 8) % 4 + (at // 2) % 4, at % 2).astype(F32)
        == target_row
    )
    at = iota((n, rows), 1)
    combine_v[...] = hot(
        slot_code(at // 32, (at // 8) % 4 + (at // 2) % 4, at % 2).astype(F32)
        == jnp.concatenate([spread(target_row)] * (rows // n), axis=1)
    )
    z0_v[pl.ds(z, 1)] = s0_v[pl.ds(z, 1)]
    wait_bytes(z0_v.at[pl.ds(0, nz - 1)], recv_sem.at[1])
    for k in range(1, ne):
        pltpu.make_async_remote_copy(
            src_ref=z0_v.at[:, lax.rem(e + k, ne)],
            dst_ref=a0_v.at[:, e],
            send_sem=send_sem.at[5],
            recv_sem=recv_sem.at[5],
            device_id=(x, at_e(k)),
            device_id_type=MESH,
        ).start()
    a0_v[:, pl.ds(e, 1)] = z0_v[:, pl.ds(e, 1)]
    wait_bytes(a0_v.at[:, pl.ds(0, ne - 1)], recv_sem.at[5])
    pair_rows = nd * 16
    level = iota((pair_rows, n), 1)
    level_of = jnp.where(level < 48, level % 16, -1).astype(F32)
    for p in range(2):
        got = a0_v[:, :, 32 + 16 * p : 48 + 16 * p, :].reshape(pair_rows, n)
        picks_v[p] = hot(got.astype(F32) == level_of)

    def widen(value, p):
        which = (iota((pair_rows, n), 0) // 2) % 2
        zero = jnp.zeros_like(value)
        xw_v[p, :, 0:n] = jnp.where(which == 0, value, zero).astype(BF)
        xw_v[p, :, n : 2 * n] = jnp.where(which == 1, value, zero).astype(BF)

    low_half = iota((rows // 16, 8, n), 1) < 4

    def swap(one, two):
        first_of = jnp.where(low_half, one, pltpu.roll(two, 4, axis=1))
        second_of = jnp.where(low_half, pltpu.roll(one, 4, axis=1), two)
        return first_of, second_of

    def first(p, c, pick=False):
        cols = slice(c * ch, (c + 1) * ch)
        layer = w1_v[c, 2 * p : 2 * p + 2].reshape(2 * n, ch)
        if pick:
            scales = mm(picks_v[p], scale_v[:, cols])
            scales_v[p, :, cols] = scales
        else:
            scales = scales_v[p, :, cols]
        u = mm(xw_v[p], layer) * scales
        h_v[p * pair_rows : (p + 1) * pair_rows, cols] = half_silu(u).astype(BF)

    def second(row, count, ranges, start, end):
        @pl.loop(0, w2_v.shape[1] // 1024)
        def _(t):
            cols = pl.ds(pl.multiple_of(t * 1024, 1024), 1024)
            part = None
            for lo, hi in ranges:
                term = mm(h_v[row : row + count, lo:hi], w2_v[lo:hi, cols])
                part = term if part is None else part + term
            if not start:
                part += acc_v[0:count, cols]
            if end:
                m_v[row : row + count, cols] = half_silu(part * 0.5).astype(BF)
            else:
                acc_v[0:count, cols] = part

    def third(p):
        total = mm(m_v[p * pair_rows : (p + 1) * pair_rows, :], outw_ref[...])
        return total.reshape(rows // 16, 8, n)

    def give_back(parts, r_v, t_v, sem):
        even, odd = swap(*parts)
        r_v[...] = jnp.stack([even, odd], axis=1).reshape(rows // 8, 8, n).astype(MSG)
        send_direct(r_v, t_v, sem)
        return mm(combine_v[...], t_v[...].reshape(rows, n).astype(BF)).astype(BF)

    for p in range(2):
        got = a0_v[:, :, 16 * p : 16 * p + 16, :]
        widen(got.reshape(pair_rows, n), p)
    w2_copy.wait()
    hid = w2_v.shape[0]
    for own in own_copies:
        own.wait()

    def span(chunks):
        return [(c * ch, (c + 1) * ch) for c in chunks]

    half = CHUNKS // 2
    for i in range(half):
        forward(i)
        first(0, to_left[i], True)
    second(0, pair_rows, [(hid // 2, hid)], True, False)
    for i in range(half, CHUNKS):
        w1_copies[1, to_left[i]].wait_recv()
        first(0, to_left[i], True)
    second(0, pair_rows, [(0, hid // 2)], False, True)
    held_v[...] = third(0)
    for i in range(half, CHUNKS):
        w1_copies[3, to_right[i]].wait_recv()
    for i in range(half):
        chunks = to_right[i], to_left[i]
        for c in chunks:
            w1_copies[2, c].wait_recv()
            first(1, c, True)
        second(pair_rows, pair_rows, span(chunks), i == 0, i == half - 1)
    values = give_back((held_v[...], third(1)), r0_v, t0_v, 2)
    features = (feats_v[...] + mm(values, back_ref[...])).astype(BF)

    q1_v[...] = mm(direct_v[...], features).reshape(rows // 8, 8, n).astype(MSG)
    send_direct(q1_v, u1_v, 3)
    got = u1_v[...].astype(F32).reshape(rows // 16, 2, 8, n)
    for p, value in enumerate(swap(got[:, 0], got[:, 1])):
        widen(value.reshape(pair_rows, n), p)
        for c in range(CHUNKS):
            first(p, c)
    second(0, rows, [(0, hid)], True, True)
    out_ref[...] = give_back((third(0), third(1)), r1_v, t1_v, 4)

    for copy in w1_copies.values():
        copy.wait_send()
    wait_bytes(x0_v.at[pl.ds(1, nx - 1)], send_sem.at[0])
    wait_bytes(z0_v.at[pl.ds(0, nz - 1)], send_sem.at[1])
    wait_bytes(a0_v.at[:, pl.ds(0, ne - 1)], send_sem.at[5])
    for dst, sem in ((t0_v, 2), (u1_v, 3), (t1_v, 4)):
        wait_bytes(dst.at[pl.ds(0, nx * nd - 1)], send_sem.at[sem])


def solution(mesh):
    nx, nd = mesh.shape["sec"], mesh.shape["dev"]
    ne = 8

    def per_device(strain, bands, damaged, owner, w1, w2, outw, scale, back):
        n, hid = w1.shape
        points = strain.shape[0]
        mid = w2.shape[1]
        rows = nd * 32
        vmem = pl.BlockSpec(memory_space=pltpu.VMEM)
        hbm = pl.BlockSpec(memory_space=pl.ANY)
        return pl.pallas_call(
            functools.partial(kernel, nx, nd, ne),
            out_shape=jax.ShapeDtypeStruct((n, outw.shape[1]), BF),
            in_specs=[hbm] * 9,
            out_specs=vmem,
            scratch_shapes=[
                pltpu.VMEM((points // n, n), jnp.int32),
                pltpu.VMEM((1, n), jnp.int32),
                pltpu.VMEM((1, n), jnp.int32),
                pltpu.VMEM(outw.shape, BF),
                pltpu.VMEM(scale.shape, F32),
                pltpu.VMEM(back.shape, BF),
                pltpu.VMEM((points, n), BF),
                pltpu.VMEM((CHUNKS, nx, n, hid // CHUNKS), BF),
                pltpu.VMEM((hid, mid), BF),
                pltpu.VMEM((n, hid), BF),
                pltpu.VMEM((2, rows // 2, hid), F32),
                pltpu.VMEM((n, points), BF),
                pltpu.VMEM((rows, nx * n), BF),
                pltpu.VMEM((n, rows), BF),
                pltpu.VMEM((rows, n), BF),
                pltpu.VMEM((2, rows // 2, n), BF),
                pltpu.VMEM((rows // 16, 8, n), F32),
                pltpu.VMEM((n, n), F32),
                pltpu.VMEM((nx, n + 16, n), BF),
                pltpu.VMEM((nd // ne, ne, 64, n), BF),
                pltpu.VMEM((nd // ne, ne, 64, n), BF),
                pltpu.VMEM((rows // 8, 8, n), MSG),
                pltpu.VMEM((nd // ne, ne, 64, n), BF),
                pltpu.VMEM((rows // 8, 8, n), MSG),
                pltpu.VMEM((2, rows // 2, 2 * n), BF),
                pltpu.VMEM((rows, hid), BF),
                pltpu.VMEM((rows // 2, mid), F32),
                pltpu.VMEM((rows, mid), BF),
                pltpu.VMEM((rows // 8, 8, n), MSG),
                pltpu.VMEM((rows // 8, 8, n), MSG),
                pltpu.VMEM((rows // 8, 8, n), MSG),
                pltpu.VMEM((rows // 8, 8, n), MSG),
                pltpu.SemaphoreType.DMA((8,)),
                pltpu.SemaphoreType.DMA((CHUNKS,)),
                pltpu.SemaphoreType.DMA((3, CHUNKS)),
                pltpu.SemaphoreType.DMA((nx, CHUNKS)),
                pltpu.SemaphoreType.DMA((6,)),
                pltpu.SemaphoreType.DMA((6,)),
            ],
            compiler_params=pltpu.CompilerParams(
                collective_id=0,
                has_side_effects=True,
                vmem_limit_bytes=62 * 2**20,
            ),
        )(
            strain,
            bands.reshape(points // n, n),
            damaged.reshape(1, n),
            owner.reshape(1, n),
            w1,
            w2,
            outw,
            scale,
            back,
        )

    both = ("sec", "dev")
    return jax.shard_map(
        per_device,
        mesh=mesh,
        in_specs=(
            P(both, None),
            P(both),
            P(both),
            P(both, None),
            P(both, None),
            P(None, "sec"),
            P("sec", None),
            P(),
            P(),
        ),
        out_specs=P(both, None),
        check_vma=False,
    )
```
